256 devices in a mesh: seq: 16 (over x_lo, y, core), head: 16 (over x_hi, z).
Axes of the slice: x: 4 (x_hi: 2, x_lo: 2; x = x_hi * 2 + x_lo), y: 4, z: 8, core: 2. Of those that a mesh axis runs over, the one named last changes fastest.
Arguments:
- tokens: bfloat16 [3072, 8192], P('seq', 'head'), may hold values from -6 to 6
- query_weight: bfloat16 [8192, 8192], P(None, 'head'), may hold values from -4 to 4
- kv_weight: bfloat16 [8192, 2048], P(None, 'head'), may hold values from -1 to 1
- signs: int32 [456, 8192], P(None, 'head'), may hold values from 0 to 262143, as said below
- cotangent: bfloat16 [3072, 8192], P('seq', 'head'), may hold values from -0.109375 to 0.109375
Outputs:
- salience: float32 [8192, 8192], P('seq', 'head')
The draws below stay inside these ranges and needn't reach their ends.
Inputs may be any that keep to these rules, and one draw needn't show every extreme that they name: `signs`: bit b of word w gives the sign of query weight row 18 w + b; bits for rows at or past 8192 are not used.
All inputs are finite; a program needn't handle non-finite values.
Results may differ from the reference program's by a relative error of at most 0.012.
The reference program's roundings to bfloat16 on the way (of `query`, `query_tangent` and `update`) count: a program that leaves them out, or rounds other values in their place, can miss the bound.
Values may be sent and summed in bfloat16 or wider, within the bound.
A program may use at most 128 MiB of HBM per device.

```python
import jax
import jax.numpy as jnp
from jax import lax

D = 8192
HD = 128
TOKENS = 3072
HQ = 64
KVH = 8
WORDS = 456


def projection_tables(key):
    key_first, key_second = jax.random.split(key)
    key_table = jax.random.normal(key_first, (D, KVH, HD), jnp.float32) * D ** (-0.5)
    value_table = jax.random.normal(key_second, (D, KVH, HD), jnp.float32) * D ** (-0.5)
    return (key_table, value_table)


def draw_query_weight(key, part):
    key = jax.random.fold_in(key, 1)
    weight_table = jax.random.normal(key, (D, HQ, HD), jnp.float32) * D ** (-0.5)
    weight_table = jnp.clip(weight_table, -4.0, 4.0)
    return weight_table.reshape(D, HQ * HD).astype(jnp.bfloat16)


def draw_kv_weight(key, part):
    key_table, value_table = projection_tables(key)
    split_keys = key_table.reshape(D, KVH, 2, HD // 2)
    split_values = value_table.reshape(D, KVH, 2, HD // 2)
    joined = jnp.stack([split_keys, split_values], axis=3)
    joined = jnp.clip(joined, -1.0, 1.0)
    return joined.reshape(D, KVH * 2 * HD).astype(jnp.bfloat16)


def draw_signs(key, part):
    key = jax.random.fold_in(key, 3)
    return jax.random.randint(key, (WORDS, HQ * HD), 0, 2 ** 18, dtype=jnp.int32)


def levels(own_key, extent, pieces, least, largest):
    def one(dim, blocks):
        draws = jax.random.uniform(jax.random.fold_in(jax.random.fold_in(own_key, 6), dim), (blocks,), jnp.float32, least / len(pieces), largest / len(pieces))
        return jnp.repeat(jnp.exp(draws), extent[dim] // blocks).reshape((-1,) + (1,) * (len(extent) - dim - 1))

    level = one(*pieces[0])
    for cut in pieces[1:]:
        level = level * one(*cut)
    return level


def bell_draw(stream_key, dims, deviation, bound, shards=(), kind=jnp.bfloat16):
    factor_of = levels(stream_key, dims, shards, -0.22, 0.18) if shards else 1.0
    values = jax.random.normal(stream_key, dims, jnp.float32) * deviation * factor_of
    return jnp.minimum(jnp.maximum(values, -bound), bound).astype(kind)


def setup_inputs(seed: int = 0) -> dict:
    keys = jax.random.split(jax.random.key(seed), 6)
    tokens = bell_draw(keys[0], (TOKENS, D), 1.0, 6.0, ((0, 16), (1, 16)))
    query_weight = draw_query_weight(jax.random.fold_in(keys[5], 71), 0)
    kv_weight = draw_kv_weight(jax.random.fold_in(keys[5], 71), 0)
    signs = draw_signs(jax.random.fold_in(keys[5], 71), 0)
    cotangent = bell_draw(keys[4], (TOKENS, HQ * HD), TOKENS ** -0.5, 0.109375, ((0, 16), (1, 16)))
    return dict(tokens=tokens, query_weight=query_weight, kv_weight=kv_weight, signs=signs, cotangent=cotangent)


def decode_signs(packed):
    shifts = jnp.arange(18, dtype=jnp.int32)
    bits = (packed[:, None, :] >> shifts[None, :, None]) & 1
    bits = bits.reshape(-1, packed.shape[1])[:D]
    return (2 * bits - 1).astype(jnp.float32)


def reference(tokens, query_weight, kv_weight, signs, cotangent):
    score_scale = HD ** -0.5
    sign_full = decode_signs(signs)
    query = jnp.dot(tokens, query_weight, preferred_element_type=jnp.float32).astype(jnp.bfloat16)
    query_tangent = jnp.dot(tokens, sign_full.astype(jnp.bfloat16), preferred_element_type=jnp.float32).astype(jnp.bfloat16)
    table = kv_weight.reshape(D, KVH, 2, 2, HD // 2)
    key_weight = table[:, :, :, 0, :].reshape(D, KVH * HD)
    value_weight = table[:, :, :, 1, :].reshape(D, KVH * HD)
    key_all = jnp.dot(tokens, key_weight, preferred_element_type=jnp.float32).astype(jnp.bfloat16)
    value_all = jnp.dot(tokens, value_weight, preferred_element_type=jnp.float32).astype(jnp.bfloat16)
    position = jnp.arange(TOKENS, dtype=jnp.int32)
    visible = position[None, :] <= position[:, None]
    group_size = HQ // KVH

    def one_head(head_index):
        group_index = head_index // group_size
        query_head = lax.dynamic_slice_in_dim(query, head_index * HD, HD, 1)
        tangent_head = lax.dynamic_slice_in_dim(query_tangent, head_index * HD, HD, 1)
        cot_head = lax.dynamic_slice_in_dim(cotangent, head_index * HD, HD, 1)
        key_head = lax.dynamic_slice_in_dim(key_all, group_index * HD, HD, 1)
        value_head = lax.dynamic_slice_in_dim(value_all, group_index * HD, HD, 1)
        logits = jnp.dot(query_head, key_head.T, preferred_element_type=jnp.float32) * score_scale
        logit_tangent = jnp.dot(tangent_head, key_head.T, preferred_element_type=jnp.float32) * score_scale
        masked = jnp.where(visible, logits, -1e30)
        row_max = jnp.max(masked, axis=1)
        weights_exp = jnp.where(visible, jnp.exp(masked - row_max[:, None]), 0.0)
        row_total = jnp.sum(weights_exp, axis=1)
        probs = weights_exp / row_total[:, None]
        centre = jnp.sum(probs * logit_tangent, axis=1)
        probs_tangent = probs * (logit_tangent - centre[:, None])
        output_sum = jnp.dot(probs.astype(jnp.bfloat16), value_head, preferred_element_type=jnp.float32)
        output_tangent = jnp.dot(probs_tangent.astype(jnp.bfloat16), value_head, preferred_element_type=jnp.float32)
        cot_float = cot_head.astype(jnp.float32)
        delta = jnp.sum(cot_float * output_sum, axis=1)
        delta_tangent = jnp.sum(cot_float * output_tangent, axis=1)
        back = jnp.dot(cot_head, value_head.T, preferred_element_type=jnp.float32)
        score_tangent = probs_tangent * (back - delta[:, None]) - probs * delta_tangent[:, None]
        update = jnp.dot(score_tangent.astype(jnp.bfloat16), key_head, preferred_element_type=jnp.float32) * score_scale
        return update.astype(jnp.bfloat16)

    updates = lax.map(one_head, jnp.arange(HQ, dtype=jnp.int32))
    update_all = updates.transpose(1, 0, 2).reshape(TOKENS, HQ * HD)
    hessian = lax.dot_general(tokens, update_all, (((0,), (0,)), ((), ())), preferred_element_type=jnp.float32)
    return sign_full * hessian
```

```python
import functools

import jax
import jax.numpy as jnp
from jax import lax
from jax.experimental import pallas as pl
from jax.experimental.pallas import tpu as pltpu
from jax.sharding import PartitionSpec as P

MESH = pl.DeviceIdType.MESH
BF16 = jnp.bfloat16
F32 = jnp.float32
BITS = 18
HEAD = 128
CHUNK = 256
LOG2E = 1.4426950408889634
PEERS = ((0, 2), (1, 0), (0, 1), (1, 2), (0, 3), (1, 1), (1, 3))


def mm(a, b):
    return jnp.dot(a, b, preferred_element_type=F32)


def mm_bt(a, b):
    return lax.dot_general(a, b, (((1,), (1,)), ((), ())), preferred_element_type=F32)


def mm_at(a, b):
    return lax.dot_general(a, b, (((0,), (0,)), ((), ())), preferred_element_type=F32)


def kernel(
    tokens_hbm, weight_hbm, kv_weight_hbm, signs_hbm, cot_hbm, out_hbm,
    tok, weight, kv_weight, words, bitmask, sign, cot, acc_q, acc_t, acc_kv,
    col, kv_own, kv_part, kv, qrows, trows, crows, buf_l, buf_t, stat, upd, out,
    load_sem, w_sem, ring_s, ring_r, xh_sem, col_s, col_r, colf_s, colf_r,
    kvx_sem, kv_s, kv_f, kv_r, upd_s, upd_f, upd_r, out_sem,
):
    rows, cols = tokens_hbm.shape
    half, quarter = rows // 2, rows // 4
    s = lax.axis_index("seq")
    h = lax.axis_index("head")
    xl, y, c = s // 8, (s // 2) % 4, s % 2
    xh, z = h // 8, h % 8
    parity = z % 2
    other_core = s + 1 - 2 * c

    def zdev(step):
        return (s, xh * 8 + (z + 8 + step) % 8)

    def rcopy(src, dst, send, recv, dev):
        return pltpu.make_async_remote_copy(
            src_ref=src, dst_ref=dst, send_sem=send, recv_sem=recv, device_id=dev, device_id_type=MESH
        )

    def seq_rows(index, count=rows, shift=0):
        return pl.ds(pl.multiple_of(index * rows + shift, 16), count)

    def feat_rows(f):
        return pl.ds(pl.multiple_of(f * cols, 512), cols)

    def block_of(a, zz):
        return ((xh + a) % 2) * 8 + (zz + 16) % 8

    def w_load(f):
        return pltpu.make_async_copy(weight_hbm.at[feat_rows(f)], weight.at[feat_rows(f)], w_sem.at[f])

    tok_load = pltpu.make_async_copy(tokens_hbm, tok.at[h], load_sem.at[0])
    words_load = pltpu.make_async_copy(signs_hbm, words, load_sem.at[1])
    kvw_load = pltpu.make_async_copy(kv_weight_hbm, kv_weight, load_sem.at[2])
    cot_load = pltpu.make_async_copy(cot_hbm, cot, load_sem.at[3])
    tok_load.start()
    words_load.start()
    w_load(h).start()
    kvw_load.start()

    @pl.loop(1, 16)
    def _(i):
        w_load((h + i) % 16).start()

    cot_load.start()

    barrier = pltpu.get_barrier_semaphore()
    xh_dev = (s, ((xh + 1) % 2) * 8 + z)
    for dev in (zdev(1), zdev(-1), xh_dev):
        pl.semaphore_signal(barrier, inc=1, device_id=dev, device_id_type=MESH)

    @pl.loop(1, 16)
    def _(i):
        pl.semaphore_signal(barrier, inc=1, device_id=((s + i) % 16, h), device_id_type=MESH)

    pl.semaphore_wait(barrier, 18)

    def ring_copy(d, k, a, full=True):
        f = block_of(a, z - (1 - 2 * d) * (k - 1))
        part = tok.at[f] if full else tok.at[f, pl.ds(pl.multiple_of(d * half, 16), half)]
        return rcopy(part, part, ring_s.at[d, k - 1, a], ring_r.at[d, k - 1, a], zdev(1 - 2 * d))

    def ring_arrival(d, k, a, full=True):
        f = block_of(a, z - (1 - 2 * d) * k)
        part = tok.at[f] if full else tok.at[f, pl.ds(pl.multiple_of(d * half, 16), half)]
        return rcopy(part, part, ring_s.at[d, k - 1, a], ring_r.at[d, k - 1, a], zdev(1 - 2 * d))

    def col_copy(f):
        return rcopy(
            tok.at[f, pl.ds(pl.multiple_of(parity * half, 16), half)],
            col.at[seq_rows(s, half, parity * half)],
            col_s.at[f], col_r.at[s], (f, h),
        )

    def col_arrival(src):
        place = col.at[seq_rows(src, half, parity * half)]
        return rcopy(place, place, col_s.at[src], col_r.at[src], (src, h))

    col_local = pltpu.make_async_copy(tok.at[s], col.at[seq_rows(s)], load_sem.at[4])

    def col_send(f):
        @pl.when(f != s)
        def _():
            col_copy(f).start()

        @pl.when(f == s)
        def _():
            col_local.start()

    def project(f):
        w_load(f).wait()
        block = tok[f]
        acc_q[...] += mm(block, weight[feat_rows(f), :])
        acc_t[...] += mm(block, sign[feat_rows(f), :])
        acc_kv[...] += mm(block, kv_weight[feat_rows(f), :])

    tok_load.wait()
    xh_copy = rcopy(tok.at[h], tok.at[h], xh_sem.at[0], xh_sem.at[1], xh_dev)
    xh_copy.start()
    ring_copy(0, 1, 0).start()
    ring_copy(1, 1, 0).start()
    col_send(h)

    acc_q[...] = jnp.zeros_like(acc_q)
    acc_t[...] = jnp.zeros_like(acc_t)
    acc_kv[...] = jnp.zeros_like(acc_kv)
    words_load.wait()
    sub = lax.broadcasted_iota(jnp.int32, (8, HEAD), 0)
    for k in range(BITS):
        shift = sub + (8 * k) % BITS
        shift = jnp.where(shift >= BITS, shift - BITS, shift)
        bitmask[8 * k : 8 * k + 8, :] = jnp.left_shift(jnp.ones_like(shift), shift)

    def decode(g, lo_k, hi_k):
        for lane in range(cols // HEAD):
            w8 = words[pl.ds(pl.multiple_of(g * 8, 8), 8), lane * HEAD : (lane + 1) * HEAD]
            for k2 in range(BITS // 2):
                parts = []
                for k in (2 * k2, 2 * k2 + 1):
                    first, last = 8 * k // BITS, (8 * k + 7) // BITS
                    word = jnp.broadcast_to(w8[first : first + 1], (8, HEAD))
                    if last != first:
                        later = jnp.broadcast_to(w8[last : last + 1], (8, HEAD))
                        word = jnp.where(sub >= BITS * last - 8 * k, later, word)
                    bit = word & bitmask[8 * k : 8 * k + 8, :]
                    parts.append(jnp.where(bit != 0, 1.0, -1.0).astype(F32))
                tile = jnp.concatenate(parts, axis=0).astype(BF16)
                at = pl.multiple_of(g * (8 * BITS) + 16 * k2, 16)
                sign[pl.ds(at, 16), lane * HEAD : (lane + 1) * HEAD] = tile

    groups = words.shape[0] // 8

    @pl.loop(0, groups)
    def _(g):
        decode(g, 0, 0)

    xh_copy.wait_recv()
    ring_copy(0, 1, 1).start()
    ring_copy(1, 1, 1).start()
    col_send(block_of(1, z))
    kvw_load.wait()

    @pl.loop(0, 2)
    def _(a):
        project(block_of(a, z))

    @pl.loop(0, 12)
    def _(m):
        k = m // 4 + 1
        a = (m // 2) % 2
        d = m % 2
        ring_arrival(d, k, a).wait_recv()

        @pl.when(k < 3)
        def _():
            ring_copy(d, k + 1, a).start()

        @pl.when(k == 3)
        def _():
            ring_copy(d, 4, a, full=False).start()

        f = block_of(a, z - (1 - 2 * d) * k)
        col_send(f)
        project(f)

    @pl.loop(0, 2)
    def _(a):
        ring_arrival(0, 4, a, full=False).wait_recv()
        ring_arrival(1, 4, a, full=False).wait_recv()
        f = block_of(a, z + 4)
        col_send(f)
        project(f)

    kv_own[...] = acc_kv[...].astype(BF16)
    kv_dev = (s, h + 1 - 2 * (h % 2))
    kvx = rcopy(kv_own, kv_part, kvx_sem.at[0], kvx_sem.at[1], kv_dev)
    kvx.start()
    cot_load.wait()
    for u in range(2):
        for j in range(2):
            lanes = slice((2 * u + j) * HEAD, (2 * u + j + 1) * HEAD)
            qrows[u, j * rows : (j + 1) * rows, :] = acc_q[:, lanes].astype(BF16)
            trows[u, j * rows : (j + 1) * rows, :] = acc_t[:, lanes].astype(BF16)
            crows[u, j * rows : (j + 1) * rows, :] = cot[:, lanes]
    kvx.wait_recv()
    odd = h % 2 == 1
    mine, theirs = kv_own[...].astype(F32), kv_part[...].astype(F32)
    lower = jnp.where(odd, theirs, mine)
    upper = jnp.where(odd, mine, theirs)
    hw = HEAD // 2
    kv[seq_rows(s), :] = jnp.concatenate(
        [lower[:, :hw], upper[:, :hw], lower[:, hw:], upper[:, hw:]], axis=1
    ).astype(BF16)

    def peer(offset):
        return ((xl + offset[0]) % 2) * 8 + ((y + offset[1]) % 4) * 2 + c

    def gather_copies(place, send, fwd, recv):
        def to(src, dev, sem):
            return rcopy(place(src), place(src), sem, recv.at[src], (dev, h))

        direct = [to(s, peer(o), send.at[i]) for i, o in enumerate(PEERS)]
        passed = [to(s, other_core, fwd.at[7])]
        passed += [to(peer(o), other_core, fwd.at[i]) for i, o in enumerate(PEERS)]
        return to, direct, passed

    def gather_start(parts):
        _, direct, passed = parts
        for copy in direct:
            copy.start()
        passed[0].start()

    def gather_pass(parts, send):
        to, _, passed = parts
        for i, o in enumerate(PEERS):
            to(peer(o), peer(o), send.at[i]).wait_recv()
            passed[i + 1].start()

    def gather_finish(parts, send):
        to, _, _ = parts
        to(other_core, other_core, send.at[0]).wait_recv()
        for i, o in enumerate(PEERS):
            to(peer(o) + 1 - 2 * c, other_core, send.at[i]).wait_recv()

    def gather_drain(parts):
        _, direct, passed = parts
        for copy in direct + passed:
            copy.wait_send()

    kv_parts = gather_copies(lambda i: kv.at[seq_rows(i)], kv_s, kv_f, kv_r)
    gather_start(kv_parts)
    gather_pass(kv_parts, kv_s)

    def colf_copy(d, src):
        place = col.at[seq_rows(src, quarter, parity * half + d * quarter)]
        return rcopy(place, place, colf_s.at[d, src], colf_r.at[d, src], zdev(1 - 2 * d))

    def colf_arrival(d, src):
        place = col.at[seq_rows(src, quarter, (1 - parity) * half + d * quarter)]
        return rcopy(place, place, colf_s.at[d, src], colf_r.at[d, src], zdev(1 - 2 * d))

    @pl.loop(1, 16)
    def _(i):
        src = (s + i) % 16
        col_arrival(src).wait_recv()
        colf_copy(0, src).start()
        colf_copy(1, src).start()

    gather_finish(kv_parts, kv_s)

    scale = HEAD ** (-0.5)
    n_rows = 2 * rows

    def attend(u, b):
        count = (rows * (b + 1) + CHUNK - 1) // CHUNK

        def keys(j):
            return kv[pl.ds(pl.multiple_of(j * CHUNK, CHUNK), CHUNK), :HEAD]

        def values(j):
            return kv[pl.ds(pl.multiple_of(j * CHUNK, CHUNK), CHUNK), HEAD:]

        stat[0] = jnp.full((n_rows, HEAD), -1e30, F32)

        @pl.loop(0, count)
        def _(j):
            key = keys(j)
            rel = lax.broadcasted_iota(jnp.int32, (rows, CHUNK), 1) - lax.broadcasted_iota(
                jnp.int32, (rows, CHUNK), 0
            )
            seen = rel <= b * rows - j * CHUNK
            logits = mm_bt(qrows[u], key)
            buf_t[j] = mm_bt(trows[u], key)
            for p in range(2):
                part = jnp.where(seen, logits[p * rows : (p + 1) * rows], -1e30)
                buf_l[j, p * rows : (p + 1) * rows, :] = part
                high = jnp.maximum(part[:, :HEAD], part[:, HEAD:])
                stat[0, p * rows : (p + 1) * rows, :] = jnp.maximum(
                    stat[0, p * rows : (p + 1) * rows, :], high
                )

        top = jnp.max(stat[0], axis=1, keepdims=True)
        stat[0] = jnp.broadcast_to(top, (n_rows, HEAD))
        stat[1] = jnp.zeros((n_rows, HEAD), F32)
        stat[2] = jnp.zeros((n_rows, HEAD), F32)

        @pl.loop(0, count)
        def _(j):
            for p in range(4):
                r = slice(p * half, (p + 1) * half)
                top = stat[0, r, :]
                total, centre = stat[1, r, :], stat[2, r, :]
                for q in range(2):
                    lanes = slice(q * HEAD, (q + 1) * HEAD)
                    e = jnp.exp2((buf_l[j, r, lanes] - top) * (scale * LOG2E))
                    buf_l[j, r, lanes] = e
                    total += e
                    centre += e * buf_t[j, r, lanes]
                stat[1, r, :] = total
                stat[2, r, :] = centre

        inverse = 1.0 / jnp.sum(stat[1], axis=1, keepdims=True)
        middle = jnp.sum(stat[2], axis=1, keepdims=True) * inverse
        stat[0] = jnp.broadcast_to(inverse, (n_rows, HEAD))
        stat[1] = jnp.broadcast_to(middle, (n_rows, HEAD))
        stat[2] = jnp.zeros((n_rows, HEAD), F32)
        stat[3] = jnp.zeros((n_rows, HEAD), F32)

        @pl.loop(0, count)
        def _(j):
            value = values(j)
            for p in range(2):
                r = slice(p * rows, (p + 1) * rows)
                inverse, middle = stat[0, r, :], stat[1, r, :]
                probs, tangents = [], []
                for q in range(2):
                    lanes = slice(q * HEAD, (q + 1) * HEAD)
                    prob = buf_l[j, r, lanes] * inverse
                    tangent = prob * ((buf_t[j, r, lanes] - middle) * scale)
                    buf_l[j, r, lanes] = prob
                    buf_t[j, r, lanes] = tangent
                    probs.append(prob.astype(BF16))
                    tangents.append(tangent.astype(BF16))
                stat[2, r, :] += mm(jnp.concatenate(probs, axis=1), value)
                stat[3, r, :] += mm(jnp.concatenate(tangents, axis=1), value)

        cot_rows = crows[u].astype(F32)
        delta = jnp.sum(cot_rows * stat[2], axis=1, keepdims=True)
        delta_t = jnp.sum(cot_rows * stat[3], axis=1, keepdims=True)
        stat[0] = jnp.broadcast_to(delta, (n_rows, HEAD))
        stat[1] = jnp.broadcast_to(delta_t, (n_rows, HEAD))
        stat[2] = jnp.zeros((n_rows, HEAD), F32)

        @pl.loop(0, count)
        def _(j):
            key, value = keys(j), values(j)
            for p in range(2):
                r = slice(p * rows, (p + 1) * rows)
                delta, delta_t = stat[0, r, :], stat[1, r, :]
                back = mm_bt(crows[u, r, :], value)
                scores = []
                for q in range(2):
                    lanes = slice(q * HEAD, (q + 1) * HEAD)
                    score = buf_t[j, r, lanes] * (back[:, lanes] - delta) - buf_l[j, r, lanes] * delta_t
                    scores.append(score.astype(BF16))
                stat[2, r, :] += mm(jnp.concatenate(scores, axis=1), key)

        update = (stat[2] * scale).astype(BF16)
        upd[u, seq_rows(b), :] = jnp.concatenate([update[:rows], update[rows:]], axis=1)

    upd_parts = []
    for u in range(2):
        attend(u, s)
        parts = gather_copies(lambda i, u=u: upd.at[u, seq_rows(i)], upd_s.at[u], upd_f.at[u], upd_r.at[u])
        gather_start(parts)
        upd_parts.append(parts)

    @pl.loop(1, 16)
    def _(i):
        src = (s + i) % 16
        colf_arrival(0, src).wait_recv()
        colf_arrival(1, src).wait_recv()

    col_local.wait()
    width = 2 * HEAD
    stores = []
    for u in range(2):
        gather_pass(upd_parts[u], upd_s.at[u])
    for u in range(2):
        gather_finish(upd_parts[u], upd_s.at[u])
        for t in range(2):
            r = slice(t * width, (t + 1) * width)
            hessian = mm_at(col[:, r], upd[u])
            own = sign[pl.ds(pl.multiple_of(s * cols + t * width, 256), width), u * width : (u + 1) * width]
            out[u, r, :] = hessian * own.astype(F32)
        store = pltpu.make_async_copy(
            out.at[u], out_hbm.at[:, pl.ds(u * width, width)], out_sem.at[u]
        )
        store.start()
        stores.append(store)

    for parts in [kv_parts] + upd_parts:
        gather_drain(parts)
    kvx.wait_send()
    xh_copy.wait_send()

    @pl.loop(0, 2)
    def _(d):
        @pl.loop(0, 2)
        def _(a):
            @pl.loop(1, 4)
            def _(k):
                ring_copy(d, k, a).wait_send()

            ring_copy(d, 4, a, full=False).wait_send()

    @pl.loop(1, 16)
    def _(i):
        other = (s + i) % 16
        col_copy(other).wait_send()
        colf_copy(0, other).wait_send()
        colf_copy(1, other).wait_send()

    for store in stores:
        store.wait()


def local(tokens, query_weight, kv_weight, signs, cotangent):
    rows, cols = tokens.shape
    width = query_weight.shape[0]
    words = signs.shape[0]
    total = 16 * rows
    chunks = total // CHUNK
    dma = pltpu.SemaphoreType.DMA
    vmem = pltpu.VMEM
    scratch = [
        vmem((16, rows, cols), BF16),
        vmem((width, cols), BF16),
        vmem((width, HEAD), BF16),
        vmem((words, cols), jnp.int32),
        vmem((8 * BITS, HEAD), jnp.int32),
        vmem((words * BITS, cols), BF16),
        vmem((rows, cols), BF16),
        vmem((rows, cols), F32),
        vmem((rows, cols), F32),
        vmem((rows, HEAD), F32),
        vmem((total, cols), BF16),
        vmem((rows, HEAD), BF16),
        vmem((rows, HEAD), BF16),
        vmem((total, 2 * HEAD), BF16),
        vmem((2, 2 * rows, HEAD), BF16),
        vmem((2, 2 * rows, HEAD), BF16),
        vmem((2, 2 * rows, HEAD), BF16),
        vmem((chunks, 2 * rows, CHUNK), F32),
        vmem((chunks, 2 * rows, CHUNK), F32),
        vmem((4, 2 * rows, HEAD), F32),
        vmem((2, total, 2 * HEAD), BF16),
        vmem((2, cols, 2 * HEAD), F32),
        dma((5,)),
        dma((16,)),
        dma((2, 4, 2)),
        dma((2, 4, 2)),
        dma((2,)),
        dma((16,)),
        dma((16,)),
        dma((2, 16)),
        dma((2, 16)),
        dma((2,)),
        dma((7,)),
        dma((8,)),
        dma((16,)),
        dma((2, 7)),
        dma((2, 8)),
        dma((2, 16)),
        dma((2,)),
    ]
    return pl.pallas_call(
        kernel,
        out_shape=jax.ShapeDtypeStruct((width // 16, cols), F32),
        in_specs=[pl.BlockSpec(memory_space=pl.ANY)] * 5,
        out_specs=pl.BlockSpec(memory_space=pl.ANY),
        scratch_shapes=scratch,
        compiler_params=pltpu.CompilerParams(
            collective_id=0, has_side_effects=True, vmem_limit_bytes=60 * 1024 * 1024
        ),
        name="salience",
    )(tokens, query_weight, kv_weight, signs, cotangent)


def solution(mesh):
    placed = (P("seq", "head"), P(None, "head"), P(None, "head"), P(None, "head"), P("seq", "head"))
    return jax.shard_map(
        local, mesh=mesh, in_specs=placed, out_specs=P("seq", "head"), check_vma=False
    )
```

```python
import functools

import jax
import jax.numpy as jnp
from jax import lax
from jax.experimental import pallas as pl
from jax.experimental.pallas import tpu as pltpu
from jax.sharding import PartitionSpec as P

MESH = pl.DeviceIdType.MESH
BF16 = jnp.bfloat16
F32 = jnp.float32
BITS = 18
HEAD = 128
CHUNK = 384
LOG2E = 1.4426950408889634


def mm(a, b):
    return jnp.dot(a, b, preferred_element_type=F32)


def mm_bt(a, b):
    return lax.dot_general(a, b, (((1,), (1,)), ((), ())), preferred_element_type=F32)


def mm_at(a, b):
    return lax.dot_general(a, b, (((0,), (0,)), ((), ())), preferred_element_type=F32)


def kernel(
    tokens_hbm, weight_hbm, kv_weight_hbm, signs_hbm, cot_hbm, out_hbm,
    tok, weight, kv_weight, words, bitmask, sign, cot, acc_q, acc_t, acc_kv,
    col, kv_own, kv_part, kv, qrows, trows, crows, buf_l, buf_t, buf_b, scores, stat, upd, out,
    load_sem, w_sem, ring_s, ring_r, xh_s, xh_r, col_s, col_r, colf_s, colf_r,
    swap_s, swap_r, kvx_sem, kv_s, kv_f, kv_r, upd_s, upd_f, upd_r, out_sem,
):
    rows, cols = tokens_hbm.shape
    half, quarter = rows // 2, rows // 4
    s = lax.axis_index("seq")
    h = lax.axis_index("head")
    xl, y, c = s // 8, (s // 2) % 4, s % 2
    xh, z = h // 8, h % 8
    parity = z % 2
    other_core = s + 1 - 2 * c

    def zdev(step):
        return (s, xh * 8 + (z + 8 + step) % 8)

    def rcopy(src, dst, send, recv, dev):
        return pltpu.make_async_remote_copy(
            src_ref=src, dst_ref=dst, send_sem=send, recv_sem=recv, device_id=dev, device_id_type=MESH
        )

    pair = 15 - s

    def part_rows(part):
        return pl.ds(pl.multiple_of(part * half, 16), half)

    def place_rows(src, part, count=half, shift=0):
        unit = (part + src // 8) % 2
        return pl.ds(pl.multiple_of((unit * 16 + src) * half + shift, 16), count)

    def feat_rows(f):
        return pl.ds(pl.multiple_of(f * cols, 512), cols)

    def block_of(a, zz):
        return ((xh + a) % 2) * 8 + (zz + 16) % 8

    def w_load(f):
        return pltpu.make_async_copy(weight_hbm.at[feat_rows(f)], weight.at[feat_rows(f)], w_sem.at[f])

    tok_load = pltpu.make_async_copy(tokens_hbm.at[part_rows(0)], tok.at[h, part_rows(0)], load_sem.at[0])
    words_load = pltpu.make_async_copy(signs_hbm, words, load_sem.at[1])
    kvw_load = pltpu.make_async_copy(kv_weight_hbm, kv_weight, load_sem.at[2])
    cot_load = pltpu.make_async_copy(cot_hbm.at[part_rows(0)], cot.at[part_rows(0)], load_sem.at[3])
    tok_load.start()
    words_load.start()
    w_load(h).start()
    kvw_load.start()

    @pl.loop(1, 16)
    def _(i):
        w_load((h + i) % 16).start()

    cot_load.start()

    barrier = pltpu.get_barrier_semaphore()
    xh_dev = (s, ((xh + 1) % 2) * 8 + z)
    for dev in (zdev(1), zdev(-1), xh_dev):
        pl.semaphore_signal(barrier, inc=1, device_id=dev, device_id_type=MESH)

    @pl.loop(1, 16)
    def _(i):
        pl.semaphore_signal(barrier, inc=1, device_id=((s + i) % 16, h), device_id_type=MESH)

    pl.semaphore_wait(barrier, 18)

    def chunk(f, part):
        return tok.at[f, part_rows(part)]

    def ring_copy(d, k, a, part):
        ref = chunk(block_of(a, z - (1 - 2 * d) * (k - 1)), part)
        return rcopy(
            ref, ref, ring_s.at[d, k - 1, a, part], ring_r.at[d, k - 1, a, part], zdev(1 - 2 * d)
        )

    def ring_arrival(d, k, a, part):
        ref = chunk(block_of(a, z - (1 - 2 * d) * k), part)
        return rcopy(
            ref, ref, ring_s.at[d, k - 1, a, part], ring_r.at[d, k - 1, a, part], zdev(1 - 2 * d)
        )

    def xh_copy(part):
        return rcopy(chunk(h, part), chunk(h, part), xh_s.at[part], xh_r.at[part], xh_dev)

    def xh_arrival(part):
        ref = chunk(block_of(1, z), part)
        return rcopy(ref, ref, xh_s.at[part], xh_r.at[part], xh_dev)

    def col_copy(f):
        return rcopy(
            chunk(f, parity),
            col.at[place_rows(s, parity)],
            col_s.at[f], col_r.at[s], (f, h),
        )

    def col_arrival(src):
        place = col.at[place_rows(src, parity)]
        return rcopy(place, place, col_s.at[src], col_r.at[src], (src, h))

    def col_local(part):
        return pltpu.make_async_copy(
            chunk(s, part), col.at[place_rows(s, part)], load_sem.at[4 + part]
        )

    def col_send(f):
        @pl.when(f != s)
        def _():
            col_copy(f).start()

    def col_keep(f):
        @pl.when(f == s)
        def _():
            col_local(0).start()
            col_local(1).start()

    tok_swap = rcopy(
        tokens_hbm.at[part_rows(1)], tok.at[h, part_rows(1)], swap_s.at[0], swap_r.at[0], (pair, h)
    )
    cot_swap = rcopy(
        cot_hbm.at[part_rows(1)], cot.at[part_rows(1)], swap_s.at[1], swap_r.at[1], (pair, h)
    )
    tok_swap.start()
    tok_load.wait()

    def own_send(part):
        xh_copy(part).start()
        ring_copy(0, 1, 0, part).start()
        ring_copy(1, 1, 0, part).start()

        @pl.when(part == parity)
        def _():
            col_send(h)

    own_send(0)
    acc_q[...] = jnp.zeros_like(acc_q)
    acc_t[...] = jnp.zeros_like(acc_t)
    acc_kv[...] = jnp.zeros_like(acc_kv)
    words_load.wait()
    sub = lax.broadcasted_iota(jnp.int32, (8, HEAD), 0)
    for k in range(BITS):
        shift = sub + (8 * k) % BITS
        shift = jnp.where(shift >= BITS, shift - BITS, shift)
        bitmask[8 * k : 8 * k + 8, :] = jnp.left_shift(jnp.ones_like(shift), shift)

    def decode_group(g):
        for lane in range(cols // HEAD):
            w8 = words[pl.ds(pl.multiple_of(g * 8, 8), 8), lane * HEAD : (lane + 1) * HEAD]
            for k2 in range(BITS // 2):
                parts = []
                for k in (2 * k2, 2 * k2 + 1):
                    first, last = 8 * k // BITS, (8 * k + 7) // BITS
                    word = jnp.broadcast_to(w8[first : first + 1], (8, HEAD))
                    if last != first:
                        later = jnp.broadcast_to(w8[last : last + 1], (8, HEAD))
                        word = jnp.where(sub >= BITS * last - 8 * k, later, word)
                    bit = word & bitmask[8 * k : 8 * k + 8, :]
                    parts.append(jnp.where(bit != 0, 1.0, -1.0).astype(F32))
                tile = jnp.concatenate(parts, axis=0).astype(BF16)
                at = pl.multiple_of(g * (8 * BITS) + 16 * k2, 16)
                sign[pl.ds(at, 16), lane * HEAD : (lane + 1) * HEAD] = tile

    def decode(f):
        low = f * cols // (8 * BITS)
        high = (f * cols + cols - 1) // (8 * BITS)

        @pl.loop(low, high + 1)
        def _(g):
            decode_group(g)

    def project_kv(f):
        acc_kv[...] += mm(tok[f], kv_weight[feat_rows(f), :])

    def project_q(f):
        w_load(f).wait()
        block = tok[f]
        acc_q[...] += mm(block, weight[feat_rows(f), :])
        acc_t[...] += mm(block, sign[feat_rows(f), :])

    def other_send(part):
        xh_arrival(part).wait_recv()
        ring_copy(0, 1, 1, part).start()
        ring_copy(1, 1, 1, part).start()

    other_send(0)
    tok_swap.wait_recv()
    own_send(1)
    col_keep(h)
    decode(h)
    other_send(1)
    cot_swap.start()
    col_send(block_of(1, z))
    col_keep(block_of(1, z))
    kvw_load.wait()
    project_kv(h)
    project_q(h)

    @pl.loop(0, 24)
    def _(m):
        k = m // 8 + 1
        a = (m // 4) % 2
        part = (m // 2) % 2
        d = m % 2
        ring_arrival(d, k, a, part).wait_recv()

        @pl.when((k < 3) | (part == d))
        def _():
            ring_copy(d, k + 1, a, part).start()

        f = block_of(a, z - (1 - 2 * d) * k)

        @pl.when(part == parity)
        def _():
            col_send(f)

        @pl.when(part == 0)
        def _():
            decode(f)

        @pl.when(part == 1)
        def _():
            col_keep(f)
            project_kv(f)
            project_q(f)

        @pl.when(m == 1)
        def _():
            decode(block_of(1, z))
            project_kv(block_of(1, z))
            project_q(block_of(1, z))

    decode(block_of(0, z + 4))
    decode(block_of(1, z + 4))

    @pl.loop(0, 2)
    def _(a):
        f = block_of(a, z + 4)
        ring_arrival(0, 4, a, 0).wait_recv()
        ring_arrival(1, 4, a, 1).wait_recv()
        project_kv(f)

    def colf_copy(d, src):
        place = col.at[place_rows(src, parity, quarter, d * quarter)]
        return rcopy(place, place, colf_s.at[d, src], colf_r.at[d, src], zdev(1 - 2 * d))

    def colf_arrival(d, src):
        place = col.at[place_rows(src, 1 - parity, quarter, d * quarter)]
        return rcopy(place, place, colf_s.at[d, src], colf_r.at[d, src], zdev(1 - 2 * d))

    away = (z + 8 - s % 8) % 8
    far = (away >= 3) & (away <= 5)

    def col_forward(when):
        @pl.when(when)
        def _():
            @pl.loop(1, 16)
            def _(i):
                src = (s + i) % 16
                col_arrival(src).wait_recv()
                colf_copy(0, src).start()
                colf_copy(1, src).start()

    kv_own[...] = acc_kv[...].astype(BF16)
    kv_dev = (s, h + 1 - 2 * (h % 2))
    kvx = rcopy(kv_own, kv_part, kvx_sem.at[0], kvx_sem.at[1], kv_dev)
    kvx.start()

    @pl.loop(0, 2)
    def _(a):
        project_q(block_of(a, z + 4))

    cot_load.wait()
    cot_swap.wait_recv()
    heads = cols // HEAD
    for u in range(2):
        at = pl.ds(pl.multiple_of((u + xl) % 2 * half, 16), half)
        for j in range(heads):
            lanes = slice(j * HEAD, (j + 1) * HEAD)
            into = slice(j * half, (j + 1) * half)
            qrows[u, into, :] = acc_q[at, lanes].astype(BF16)
            trows[u, into, :] = acc_t[at, lanes].astype(BF16)
            crows[u, into, :] = cot[at, lanes]
    kvx.wait_recv()
    odd = h % 2 == 1
    mine, theirs = kv_own[...].astype(F32), kv_part[...].astype(F32)
    lower = jnp.where(odd, theirs, mine)
    upper = jnp.where(odd, mine, theirs)
    hw = HEAD // 2
    kv[s] = jnp.concatenate(
        [lower[:, :hw], upper[:, :hw], lower[:, hw:], upper[:, hw:]], axis=1
    ).astype(BF16)

    x_peer = (xl + 1) % 2 * 8 + y * 2 + c

    def y_peer(step):
        return xl * 8 + (y + step) % 4 * 2 + c

    def xy_peer(step):
        return (xl + 1) % 2 * 8 + (y + step) % 4 * 2 + c

    class Gather:
        def __init__(self, place, send, fwd, recv):
            self.place, self.send, self.fwd, self.recv = place, send, fwd, recv

        def to(self, src, dev, sem):
            return rcopy(self.place(src), self.place(src), sem, self.recv.at[src], (dev, h))

        def arrived(self, src):
            self.to(src, x_peer, self.send.at[0]).wait_recv()

        def share(self, src):
            self.to(src, other_core, self.fwd.at[src // 2]).start()

        def start(self):
            self.to(s, x_peer, self.send.at[0]).start()
            for step in (2, 1, 3):
                self.to(s, y_peer(step), self.send.at[step]).start()
            self.share(s)

        def middle(self):
            @pl.when(c == 0)
            def _():
                self.arrived(x_peer)
                for i, step in enumerate((2, 1, 3)):
                    self.to(x_peer, y_peer(step), self.send.at[4 + i]).start()
                self.share(x_peer)

            @pl.when(c == 1)
            def _():
                for i, step in enumerate((1, 3, 2)):
                    self.arrived(y_peer(step))
                    self.to(y_peer(step), x_peer, self.send.at[4 + i]).start()
                    self.share(y_peer(step))

        def end(self):
            @pl.when(c == 0)
            def _():
                for step in (1, 3, 2):
                    self.arrived(y_peer(step))
                    self.share(y_peer(step))

            @pl.when(c == 1)
            def _():
                self.arrived(x_peer)
                self.share(x_peer)

            for step in (1, 3, 2):
                self.arrived(xy_peer(step))
                self.share(xy_peer(step))

        def finish(self):
            for step in range(4):
                self.arrived(y_peer(step) + 1 - 2 * c)
                self.arrived(xy_peer(step) + 1 - 2 * c)

        def drain(self):
            for i in range(7):
                self.to(s, x_peer, self.send.at[i]).wait_send()
            for i in range(8):
                self.to(s, other_core, self.fwd.at[i]).wait_send()

    kv_gather = Gather(lambda src: kv.at[src], kv_s, kv_f, kv_r)
    kv_gather.start()

    @pl.loop(0, 2)
    def _(a):
        col_send(block_of(a, z + 4))
        col_keep(block_of(a, z + 4))

    kv_gather.middle()
    col_forward(jnp.logical_not(far))
    kv_gather.end()
    col_forward(far)
    kv_gather.finish()

    scale = HEAD ** (-0.5)
    n_rows = heads * half
    pieces = CHUNK // half
    tiles = CHUNK // HEAD

    def attend(u, b, hook):
        count = (b + pieces) // pieces

        def load(j, lanes):
            parts = []
            for i in range(pieces // 2):
                owner = j * (pieces // 2) + i
                parts += [kv[owner, :half, lanes], kv[15 - owner, half:, lanes]]
            return jnp.concatenate(parts, axis=0)

        key_lanes, value_lanes = slice(0, HEAD), slice(HEAD, 2 * HEAD)
        runs = [slice(p * half, (p + 1) * half) for p in range(heads)]
        strips = [slice(q * HEAD, (q + 1) * HEAD) for q in range(tiles)]

        def logits_of(j, last):
            buf_l[j] = mm_bt(qrows[u], load(j, key_lanes))
            if last:
                rel = lax.broadcasted_iota(jnp.int32, (half, CHUNK), 1) - lax.broadcasted_iota(
                    jnp.int32, (half, CHUNK), 0
                )
                seen = rel <= b * half - j * CHUNK
            for r in runs:
                if last:
                    buf_l[j, r, :] = jnp.where(seen, buf_l[j, r, :], -1e30)
                high = stat[0, r, :]
                for lanes in strips:
                    high = jnp.maximum(high, buf_l[j, r, lanes])
                stat[0, r, :] = high

        stat[0] = jnp.full((n_rows, HEAD), -1e30, F32)

        @pl.loop(0, count - 1)
        def _(j):
            logits_of(j, False)

        logits_of(count - 1, True)
        stat[0] = jnp.broadcast_to(jnp.max(stat[0], axis=1, keepdims=True), (n_rows, HEAD))
        for i in range(1, 5):
            stat[i] = jnp.zeros((n_rows, HEAD), F32)

        @pl.loop(0, count)
        def _(j):
            buf_t[j] = mm_bt(trows[u], load(j, key_lanes))
            buf_b[j] = mm_bt(crows[u], load(j, value_lanes))
            for r in runs:
                top = stat[0, r, :]
                sums = [stat[i, r, :] for i in range(1, 5)]
                for lanes in strips:
                    e = jnp.exp2((buf_l[j, r, lanes] - top) * (scale * LOG2E))
                    buf_l[j, r, lanes] = e
                    back = buf_b[j, r, lanes]
                    et = e * buf_t[j, r, lanes]
                    for i, term in enumerate((e, et, e * back, et * back)):
                        sums[i] += term
                for i in range(4):
                    stat[i + 1, r, :] = sums[i]

        hook()
        sums = [jnp.sum(stat[i], axis=1, keepdims=True) for i in range(1, 5)]
        inverse = 1.0 / sums[0]
        middle = sums[1] * inverse
        delta = sums[2] * inverse
        delta_t = sums[3] * inverse - middle * delta
        for i, value in enumerate((middle, delta, delta_t)):
            stat[i] = jnp.broadcast_to(value, (n_rows, HEAD))
        stat[3] = jnp.zeros((n_rows, HEAD), F32)

        @pl.loop(0, count)
        def _(j):
            for r in runs:
                middle, delta, delta_t = stat[0, r, :], stat[1, r, :], stat[2, r, :]
                for lanes in strips:
                    score = buf_l[j, r, lanes] * (
                        (buf_t[j, r, lanes] - middle) * (buf_b[j, r, lanes] - delta) - delta_t
                    )
                    scores[r, lanes] = score.astype(BF16)
            stat[3] += mm(scores[...], load(j, key_lanes))

        update = (stat[3] * (inverse * (scale * scale))).astype(BF16)
        upd[upd_rows(u, s), :] = jnp.concatenate(
            [update[p * half : (p + 1) * half] for p in range(heads)], axis=1
        )

    def upd_rows(u, src):
        return pl.ds(pl.multiple_of((u * 16 + src) * half, 16), half)

    early = jnp.minimum(2 * s, 31 - 2 * s)
    gathers = [
        Gather(lambda src, u=u: upd.at[upd_rows(u, src)], upd_s.at[u], upd_f.at[u], upd_r.at[u])
        for u in range(2)
    ]
    attend(0, early, lambda: None)
    gathers[0].start()
    attend(1, 31 - early, gathers[0].middle)
    gathers[1].start()
    gathers[0].end()
    gathers[1].middle()
    gathers[0].finish()

    @pl.loop(1, 16)
    def _(i):
        src = (s + i) % 16
        colf_arrival(0, src).wait_recv()
        colf_arrival(1, src).wait_recv()

    col_local(0).wait()
    col_local(1).wait()
    side = 16 * half

    def hessian(u, t):
        run = slice(u * side, (u + 1) * side)
        return mm_at(col[run, t * 256 : (t + 1) * 256], upd[run, :])

    for t in range(cols // 256):
        out[t * 256 : (t + 1) * 256, :] = hessian(0, t)
    gathers[1].end()
    gathers[1].finish()
    stores = []
    for t in range(cols // 256):
        r = slice(t * 256, (t + 1) * 256)
        own = sign[pl.ds(pl.multiple_of(s * cols + t * 256, 256), 256), :]
        out[r, :] = (out[r, :] + hessian(1, t)) * own.astype(F32)
        store = pltpu.make_async_copy(out.at[r], out_hbm.at[r], out_sem.at[t])
        store.start()
        stores.append(store)

    for gather in [kv_gather] + gathers:
        gather.drain()
    tok_swap.wait_send()
    cot_swap.wait_send()
    kvx.wait_send()
    for part in range(2):
        xh_copy(part).wait_send()

    @pl.loop(0, 2)
    def _(d):
        @pl.loop(0, 2)
        def _(a):
            @pl.loop(1, 4)
            def _(k):
                ring_copy(d, k, a, 0).wait_send()
                ring_copy(d, k, a, 1).wait_send()

            ring_copy(d, 4, a, d).wait_send()

    @pl.loop(1, 16)
    def _(i):
        other = (s + i) % 16
        col_copy(other).wait_send()
        colf_copy(0, other).wait_send()
        colf_copy(1, other).wait_send()

    for store in stores:
        store.wait()


def local(tokens, query_weight, kv_weight, signs, cotangent):
    rows, cols = tokens.shape
    width = query_weight.shape[0]
    words = signs.shape[0]
    total = 16 * rows
    chunks = total // CHUNK
    dma = pltpu.SemaphoreType.DMA
    vmem = pltpu.VMEM
    scratch = [
        vmem((16, rows, cols), BF16),
        vmem((width, cols), BF16),
        vmem((width, HEAD), BF16),
        vmem((words, cols), jnp.int32),
        vmem((8 * BITS, HEAD), jnp.int32),
        vmem((words * BITS, cols), BF16),
        vmem((rows, cols), BF16),
        vmem((rows, cols), F32),
        vmem((rows, cols), F32),
        vmem((rows, HEAD), F32),
        vmem((total, cols), BF16),
        vmem((rows, HEAD), BF16),
        vmem((rows, HEAD), BF16),
        vmem((16, rows, 2 * HEAD), BF16),
        vmem((2, 2 * rows, HEAD), BF16),
        vmem((2, 2 * rows, HEAD), BF16),
        vmem((2, 2 * rows, HEAD), BF16),
        vmem((chunks, 2 * rows, CHUNK), F32),
        vmem((chunks, 2 * rows, CHUNK), F32),
        vmem((chunks, 2 * rows, CHUNK), F32),
        vmem((2 * rows, CHUNK), BF16),
        vmem((5, 2 * rows, HEAD), F32),
        vmem((total, cols), BF16),
        vmem((cols, cols), F32),
        dma((6,)),
        dma((16,)),
        dma((2, 4, 2, 2)),
        dma((2, 4, 2, 2)),
        dma((2,)),
        dma((2,)),
        dma((16,)),
        dma((16,)),
        dma((2, 16)),
        dma((2, 16)),
        dma((2,)),
        dma((2,)),
        dma((2,)),
        dma((7,)),
        dma((8,)),
        dma((16,)),
        dma((2, 7)),
        dma((2, 8)),
        dma((2, 16)),
        dma((2,)),
    ]
    return pl.pallas_call(
        kernel,
        out_shape=jax.ShapeDtypeStruct((width // 16, cols), F32),
        in_specs=[pl.BlockSpec(memory_space=pl.ANY)] * 5,
        out_specs=pl.BlockSpec(memory_space=pl.ANY),
        scratch_shapes=scratch,
        compiler_params=pltpu.CompilerParams(
            collective_id=0, has_side_effects=True, vmem_limit_bytes=60 * 1024 * 1024
        ),
        name="salience",
    )(tokens, query_weight, kv_weight, signs, cotangent)


def solution(mesh):
    placed = (P("seq", "head"), P(None, "head"), P(None, "head"), P(None, "head"), P("seq", "head"))
    return jax.shard_map(
        local, mesh=mesh, in_specs=placed, out_specs=P("seq", "head"), check_vma=False
    )
```

```python
import functools

import jax
import jax.numpy as jnp
from jax import lax
from jax.experimental import pallas as pl
from jax.experimental.pallas import tpu as pltpu
from jax.sharding import PartitionSpec as P

MESH = pl.DeviceIdType.MESH
BF16 = jnp.bfloat16
F32 = jnp.float32
BITS = 18
HEAD = 128
CHUNK = 384
LOG2E = 1.4426950408889634


def mm(a, b):
    return jnp.dot(a, b, preferred_element_type=F32)


def mm_bt(a, b):
    return lax.dot_general(a, b, (((1,), (1,)), ((), ())), preferred_element_type=F32)


def mm_at(a, b):
    return lax.dot_general(a, b, (((0,), (0,)), ((), ())), preferred_element_type=F32)


def kernel(
    tokens_hbm, weight_hbm, kv_weight_hbm, signs_hbm, cot_hbm, out,
    tok, weight, kv_weight, words, bitmask, sign, cot, acc_q, acc_t, acc_kv,
    col, kv, whole, qrows, trows, crows, buf_l, buf_t, buf_b, scores, stat, acc_u, upd,
    load_sem, w_sem, ring_s, ring_r, xh_s, xh_r, col_s, col_r, colf_s, colf_r,
    swap_s, swap_r, kvx_sem, kv_s, kv_f, kv_r, upd_s, upd_f, upd_r,
):
    rows, cols = tokens_hbm.shape
    half, quarter = rows // 2, rows // 4
    s = lax.axis_index("seq")
    h = lax.axis_index("head")
    xl, y, c = s // 8, (s // 2) % 4, s % 2
    xh, z = h // 8, h % 8
    parity = z % 2
    other_core = s + 1 - 2 * c

    def zdev(step):
        return (s, xh * 8 + (z + 8 + step) % 8)

    def rcopy(src, dst, send, recv, dev):
        return pltpu.make_async_remote_copy(
            src_ref=src, dst_ref=dst, send_sem=send, recv_sem=recv, device_id=dev, device_id_type=MESH
        )

    pair = 15 - s

    def part_rows(part):
        return pl.ds(pl.multiple_of(part * half, 16), half)

    def place_rows(src, part, count=half, shift=0):
        unit = (part + src // 8) % 2
        return pl.ds(pl.multiple_of((unit * 16 + src) * half + shift, 16), count)

    def feat_rows(f):
        return pl.ds(pl.multiple_of(f * cols, 512), cols)

    def block_of(a, zz):
        return ((xh + a) % 2) * 8 + (zz + 16) % 8

    barrier = pltpu.get_barrier_semaphore()
    xh_dev = (s, ((xh + 1) % 2) * 8 + z)
    for dev in (zdev(1), zdev(-1), xh_dev):
        pl.semaphore_signal(barrier, inc=1, device_id=dev, device_id_type=MESH)

    @pl.loop(1, 16)
    def _(i):
        pl.semaphore_signal(barrier, inc=1, device_id=((s + i) % 16, h), device_id_type=MESH)

    def w_load(f):
        return pltpu.make_async_copy(weight_hbm.at[feat_rows(f)], weight.at[feat_rows(f)], w_sem.at[f])

    tok_load = pltpu.make_async_copy(tokens_hbm.at[part_rows(0)], tok.at[h, part_rows(0)], load_sem.at[0])
    words_load = pltpu.make_async_copy(signs_hbm, words, load_sem.at[1])
    kvw_load = pltpu.make_async_copy(kv_weight_hbm, kv_weight, load_sem.at[2])
    cot_load = pltpu.make_async_copy(cot_hbm.at[part_rows(0)], cot.at[part_rows(0)], load_sem.at[3])
    tok_load.start()
    words_load.start()
    w_load(h).start()
    kvw_load.start()

    @pl.loop(1, 16)
    def _(i):
        w_load((h + i) % 16).start()

    cot_load.start()

    pl.semaphore_wait(barrier, 18)

    def chunk(f, part):
        return tok.at[f, part_rows(part)]

    def ring_copy(d, k, a, part):
        ref = chunk(block_of(a, z - (1 - 2 * d) * (k - 1)), part)
        return rcopy(
            ref, ref, ring_s.at[d, k - 1, a, part], ring_r.at[d, k - 1, a, part], zdev(1 - 2 * d)
        )

    def ring_arrival(d, k, a, part):
        ref = chunk(block_of(a, z - (1 - 2 * d) * k), part)
        return rcopy(
            ref, ref, ring_s.at[d, k - 1, a, part], ring_r.at[d, k - 1, a, part], zdev(1 - 2 * d)
        )

    def xh_copy(part):
        return rcopy(chunk(h, part), chunk(h, part), xh_s.at[part], xh_r.at[part], xh_dev)

    def xh_arrival(part):
        ref = chunk(block_of(1, z), part)
        return rcopy(ref, ref, xh_s.at[part], xh_r.at[part], xh_dev)

    def col_copy(f):
        return rcopy(
            chunk(f, parity),
            col.at[place_rows(s, parity)],
            col_s.at[f], col_r.at[s], (f, h),
        )

    def col_arrival(src):
        place = col.at[place_rows(src, parity)]
        return rcopy(place, place, col_s.at[src], col_r.at[src], (src, h))

    def col_local(part):
        return pltpu.make_async_copy(
            chunk(s, part), col.at[place_rows(s, part)], load_sem.at[4 + part]
        )

    def col_send(f):
        @pl.when(f != s)
        def _():
            col_copy(f).start()

    def col_keep(f):
        @pl.when(f == s)
        def _():
            col_local(0).start()
            col_local(1).start()

    tok_swap = rcopy(
        tokens_hbm.at[part_rows(1)], tok.at[h, part_rows(1)], swap_s.at[0], swap_r.at[0], (pair, h)
    )
    cot_swap = rcopy(
        cot_hbm.at[part_rows(1)], cot.at[part_rows(1)], swap_s.at[1], swap_r.at[1], (pair, h)
    )
    tok_swap.start()
    tok_load.wait()

    def own_send(part):
        xh_copy(part).start()
        ring_copy(0, 1, 0, part).start()
        ring_copy(1, 1, 0, part).start()

        @pl.when(part == parity)
        def _():
            col_send(h)

    own_send(0)
    acc_q[...] = jnp.zeros_like(acc_q)
    acc_t[...] = jnp.zeros_like(acc_t)
    acc_kv[...] = jnp.zeros_like(acc_kv)
    words_load.wait()
    sub = lax.broadcasted_iota(jnp.int32, (8, HEAD), 0)
    for k in range(BITS):
        shift = sub + (8 * k) % BITS
        shift = jnp.where(shift >= BITS, shift - BITS, shift)
        bitmask[8 * k : 8 * k + 8, :] = jnp.left_shift(jnp.ones_like(shift), shift)

    def decode_group(g):
        for lane in range(cols // HEAD):
            w8 = words[pl.ds(pl.multiple_of(g * 8, 8), 8), lane * HEAD : (lane + 1) * HEAD]
            for k2 in range(BITS // 2):
                parts = []
                for k in (2 * k2, 2 * k2 + 1):
                    first, last = 8 * k // BITS, (8 * k + 7) // BITS
                    word = jnp.broadcast_to(w8[first : first + 1], (8, HEAD))
                    if last != first:
                        later = jnp.broadcast_to(w8[last : last + 1], (8, HEAD))
                        word = jnp.where(sub >= BITS * last - 8 * k, later, word)
                    bit = word & bitmask[8 * k : 8 * k + 8, :]
                    parts.append(jnp.where(bit != 0, 1.0, -1.0).astype(F32))
                tile = jnp.concatenate(parts, axis=0).astype(BF16)
                at = pl.multiple_of(g * (8 * BITS) + 16 * k2, 16)
                sign[pl.ds(at, 16), lane * HEAD : (lane + 1) * HEAD] = tile

    def decode(f):
        low = f * cols // (8 * BITS)
        high = (f * cols + cols - 1) // (8 * BITS)

        @pl.loop(low, high + 1)
        def _(g):
            decode_group(g)

    def project_kv(f):
        acc_kv[...] += mm(tok[f], kv_weight[feat_rows(f), :])

    def project_q(f):
        w_load(f).wait()
        block = tok[f]
        acc_q[...] += mm(block, weight[feat_rows(f), :])
        acc_t[...] += mm(block, sign[feat_rows(f), :])

    def other_send(part):
        xh_arrival(part).wait_recv()
        ring_copy(0, 1, 1, part).start()
        ring_copy(1, 1, 1, part).start()

    other_send(0)
    tok_swap.wait_recv()
    own_send(1)
    col_keep(h)
    decode(h)
    other_send(1)
    cot_swap.start()
    col_send(block_of(1, z))
    col_keep(block_of(1, z))
    kvw_load.wait()
    project_kv(h)
    project_q(h)

    @pl.loop(0, 24)
    def _(m):
        k = m // 8 + 1
        part = (m // 4) % 2
        a = (m // 2) % 2
        d = m % 2
        ring_arrival(d, k, a, part).wait_recv()

        @pl.when((k < 3) | (part == d))
        def _():
            ring_copy(d, k + 1, a, part).start()

        f = block_of(a, z - (1 - 2 * d) * k)

        @pl.when(part == parity)
        def _():
            col_send(f)

        @pl.when(part == 0)
        def _():
            decode(f)

        @pl.when(part == 1)
        def _():
            col_keep(f)
            project_kv(f)
            project_q(f)

        @pl.when(m == 1)
        def _():
            decode(block_of(1, z))
            project_kv(block_of(1, z))
            project_q(block_of(1, z))

    decode(block_of(0, z + 4))
    decode(block_of(1, z + 4))

    @pl.loop(0, 2)
    def _(a):
        f = block_of(a, z + 4)
        ring_arrival(0, 4, a, 0).wait_recv()
        ring_arrival(1, 4, a, 1).wait_recv()
        project_kv(f)

    def colf_copy(d, src):
        place = col.at[place_rows(src, parity, quarter, d * quarter)]
        return rcopy(place, place, colf_s.at[d, src], colf_r.at[d, src], zdev(1 - 2 * d))

    def colf_arrival(d, src):
        place = col.at[place_rows(src, 1 - parity, quarter, d * quarter)]
        return rcopy(place, place, colf_s.at[d, src], colf_r.at[d, src], zdev(1 - 2 * d))

    away = (z + 8 - s % 8) % 8
    far = (away >= 3) & (away <= 5)

    def col_forward(when):
        @pl.when(when)
        def _():
            @pl.loop(1, 16)
            def _(i):
                src = (s + i) % 16
                col_arrival(src).wait_recv()
                colf_copy(0, src).start()
                colf_copy(1, src).start()

    x_peer = (xl + 1) % 2 * 8 + y * 2 + c

    def y_peer(step):
        return xl * 8 + (y + step) % 4 * 2 + c

    def xy_peer(step):
        return (xl + 1) % 2 * 8 + (y + step) % 4 * 2 + c

    class Gather:
        def __init__(self, place, send, fwd, recv):
            self.place, self.send, self.fwd, self.recv = place, send, fwd, recv

        def to(self, src, dev, i, p):
            ref = self.place(src, p)
            return rcopy(ref, ref, self.send.at[i, p], self.recv.at[src, p], (dev, h))

        def arrived(self, src, p):
            self.to(src, x_peer, 0, p).wait_recv()

        def share(self, src, p):
            ref = self.place(src, p)
            rcopy(ref, ref, self.fwd.at[src // 2, p], self.recv.at[src, p], (other_core, h)).start()

        def start(self, pieces=(0, 1)):
            def along_x():
                for p in pieces:
                    self.to(s, x_peer, 0, p).start()

            def along_y():
                for p in pieces:
                    for step in (1, 3, 2):
                        self.to(s, y_peer(step), step, p).start()
                    self.share(s, p)

            @pl.when(c == 0)
            def _():
                along_x()
                along_y()

            @pl.when(c == 1)
            def _():
                along_y()
                along_x()

        def middle(self, p):
            @pl.when(c == 0)
            def _():
                self.arrived(x_peer, p)
                for i, step in enumerate((1, 3, 2)):
                    self.to(x_peer, y_peer(step), 4 + i, p).start()
                self.share(x_peer, p)

            @pl.when(c == 1)
            def _():
                for i, step in enumerate((1, 3, 2)):
                    self.arrived(y_peer(step), p)
                    self.to(y_peer(step), x_peer, 4 + i, p).start()
                    self.share(y_peer(step), p)

        def end(self, p):
            @pl.when(c == 0)
            def _():
                for step in (1, 3, 2):
                    self.arrived(y_peer(step), p)
                    self.share(y_peer(step), p)

            @pl.when(c == 1)
            def _():
                self.arrived(x_peer, p)
                self.share(x_peer, p)

            for step in (1, 3, 2):
                self.arrived(xy_peer(step), p)
                self.share(xy_peer(step), p)

        def finish(self, p):
            for step in range(4):
                self.arrived(y_peer(step) + 1 - 2 * c, p)
                self.arrived(xy_peer(step) + 1 - 2 * c, p)

        def drain(self):
            for p in range(2):
                for i in range(7):
                    self.to(s, x_peer, i, p).wait_send()
                ref = self.place(s, p)
                for i in range(8):
                    rcopy(ref, ref, self.fwd.at[i, p], self.recv.at[s, p], (other_core, h)).wait_send()

    odd = h % 2
    kv[odd, s] = acc_kv[...].astype(BF16)
    kvx = rcopy(
        kv.at[odd, s], kv.at[odd, s], kvx_sem.at[0], kvx_sem.at[1], (s, h + 1 - 2 * odd)
    )
    kvx_arrival = rcopy(
        kv.at[1 - odd, s], kv.at[1 - odd, s], kvx_sem.at[0], kvx_sem.at[1], (s, h + 1 - 2 * odd)
    )
    kv_gather = Gather(lambda src, p: kv.at[(odd + p) % 2, src], kv_s, kv_f, kv_r)
    kvx.start()
    kv_gather.start((0,))

    @pl.loop(0, 2)
    def _(a):
        project_q(block_of(a, z + 4))

    kvx_arrival.wait_recv()
    kv_gather.start((1,))
    kv_gather.middle(0)

    cot_load.wait()
    cot_swap.wait_recv()
    heads = cols // HEAD
    def fill_rows(u):
        at = pl.ds(pl.multiple_of((u + xl) % 2 * half, 16), half)
        for j in range(heads):
            lanes = slice(j * HEAD, (j + 1) * HEAD)
            into = slice(j * half, (j + 1) * half)
            qrows[u, into, :] = acc_q[at, lanes].astype(BF16)
            trows[u, into, :] = acc_t[at, lanes].astype(BF16)
            crows[u, into, :] = cot[at, lanes]

    fill_rows(0)
    kv_gather.middle(1)
    kv_gather.end(0)

    @pl.loop(0, 2)
    def _(a):
        col_send(block_of(a, z + 4))
        col_keep(block_of(a, z + 4))

    fill_rows(1)
    kv_gather.end(1)
    col_forward(jnp.logical_not(far))
    kv_gather.finish(0)
    kv_gather.finish(1)
    col_forward(far)

    low = lax.broadcasted_iota(jnp.int32, (rows, HEAD), 1) < HEAD // 2

    def turned(block):
        return jnp.concatenate([block[:, HEAD // 2 :], block[:, : HEAD // 2]], axis=1)

    @pl.loop(0, 16)
    def _(src):
        lower, upper = kv[0, src].astype(F32), kv[1, src].astype(F32)
        whole[0, src] = jnp.where(low, lower, turned(upper)).astype(BF16)
        whole[1, src] = jnp.where(low, turned(lower), upper).astype(BF16)

    scale = HEAD ** (-0.5)
    n_rows = heads * half
    pieces = CHUNK // half
    tiles = CHUNK // HEAD

    def attend(u, b, hook_sums, hook_half):
        count = (b + pieces) // pieces

        def load(j, which):
            parts = []
            for i in range(pieces // 2):
                owner = j * (pieces // 2) + i
                for src, at in ((owner, slice(0, half)), (15 - owner, slice(half, rows))):
                    parts.append(whole[which, src, at])
            return jnp.concatenate(parts, axis=0)

        keys, values = 0, 1
        runs = [slice(p * half, (p + 1) * half) for p in range(heads)]
        strips = [slice(q * HEAD, (q + 1) * HEAD) for q in range(tiles)]

        def logits_of(j, last):
            buf_l[j] = mm_bt(qrows[u], load(j, keys))
            if last:
                rel = lax.broadcasted_iota(jnp.int32, (half, CHUNK), 1) - lax.broadcasted_iota(
                    jnp.int32, (half, CHUNK), 0
                )
                seen = rel <= b * half - j * CHUNK
            for r in runs:
                if last:
                    buf_l[j, r, :] = jnp.where(seen, buf_l[j, r, :], -1e30)
                high = stat[0, r, :]
                for lanes in strips:
                    high = jnp.maximum(high, buf_l[j, r, lanes])
                stat[0, r, :] = high

        stat[0] = jnp.full((n_rows, HEAD), -1e30, F32)

        @pl.loop(0, count - 1)
        def _(j):
            logits_of(j, False)

        logits_of(count - 1, True)
        stat[0] = jnp.broadcast_to(jnp.max(stat[0], axis=1, keepdims=True), (n_rows, HEAD))
        for i in range(1, 5):
            stat[i] = jnp.zeros((n_rows, HEAD), F32)

        @pl.loop(0, count)
        def _(j):
            buf_t[j] = mm_bt(trows[u], load(j, keys))
            buf_b[j] = mm_bt(crows[u], load(j, values))
            for r in runs:
                top = stat[0, r, :]
                sums = [stat[i, r, :] for i in range(1, 5)]
                for lanes in strips:
                    e = jnp.exp2((buf_l[j, r, lanes] - top) * (scale * LOG2E))
                    buf_l[j, r, lanes] = e
                    back = buf_b[j, r, lanes]
                    et = e * buf_t[j, r, lanes]
                    for i, term in enumerate((e, et, e * back, et * back)):
                        sums[i] += term
                for i in range(4):
                    stat[i + 1, r, :] = sums[i]

        hook_sums()
        sums = [jnp.sum(stat[i], axis=1, keepdims=True) for i in range(1, 5)]
        inverse = 1.0 / sums[0]
        middle = sums[1] * inverse
        delta = sums[2] * inverse
        delta_t = sums[3] * inverse - middle * delta
        for i, value in enumerate((middle, delta, delta_t)):
            stat[i] = jnp.broadcast_to(value, (n_rows, HEAD))
        acc_u[...] = jnp.zeros_like(acc_u)

        factor = inverse * (scale * scale)
        for p in range(2):
            both = slice(p * n_rows // 2, (p + 1) * n_rows // 2)

            @pl.loop(0, count)
            def _(j):
                for r in runs[2 * p : 2 * p + 2]:
                    middle, delta, delta_t = stat[0, r, :], stat[1, r, :], stat[2, r, :]
                    for lanes in strips:
                        score = buf_l[j, r, lanes] * (
                            (buf_t[j, r, lanes] - middle) * (buf_b[j, r, lanes] - delta) - delta_t
                        )
                        scores[r, lanes] = score.astype(BF16)
                acc_u[both, :] += mm(scores[both, :], load(j, keys))

            update = (acc_u[both, :] * factor[both]).astype(BF16)
            upd[p, upd_rows(u, s), :] = jnp.concatenate([update[:half], update[half:]], axis=1)
            hook_half(p)

    def upd_rows(u, src):
        return pl.ds(pl.multiple_of((u * 16 + src) * half, 16), half)

    early = jnp.minimum(2 * s, 31 - 2 * s)
    gathers = [
        Gather(lambda src, p, u=u: upd.at[p, upd_rows(u, src)], upd_s.at[u], upd_f.at[u], upd_r.at[u])
        for u in range(2)
    ]

    def first_middle():
        gathers[0].middle(0)
        gathers[0].middle(1)

    attend(0, early, lambda: None, lambda p: gathers[0].start((p,)))
    attend(1, 31 - early, first_middle, lambda p: gathers[1].start((p,)))
    gathers[0].end(0)
    gathers[1].middle(0)
    gathers[0].end(1)
    gathers[1].middle(1)
    gathers[0].finish(0)
    gathers[0].finish(1)

    @pl.loop(1, 16)
    def _(i):
        src = (s + i) % 16
        colf_arrival(0, src).wait_recv()
        colf_arrival(1, src).wait_recv()

    col_local(0).wait()
    col_local(1).wait()
    side = 16 * half

    width = cols // 2

    def hessian(u, t, p):
        run = slice(u * side, (u + 1) * side)
        return mm_at(col[run, t * 256 : (t + 1) * 256], upd[p, run, :])

    places = [
        (t, p, slice(t * 256, (t + 1) * 256), slice(p * width, (p + 1) * width))
        for p in range(2)
        for t in range(cols // 256)
    ]
    for t, p, r, lanes in places:
        out[r, lanes] = hessian(0, t, p)
    for p in range(2):
        gathers[1].end(p)
    for p in range(2):
        gathers[1].finish(p)
        for t, q, r, lanes in places:
            if p == q:
                own = sign[pl.ds(pl.multiple_of(s * cols + t * 256, 256), 256), lanes]
                out[r, lanes] = (out[r, lanes] + hessian(1, t, p)) * own.astype(F32)

    for gather in [kv_gather] + gathers:
        gather.drain()
    tok_swap.wait_send()
    cot_swap.wait_send()
    kvx.wait_send()
    for part in range(2):
        xh_copy(part).wait_send()

    @pl.loop(0, 2)
    def _(d):
        @pl.loop(0, 2)
        def _(a):
            @pl.loop(1, 4)
            def _(k):
                ring_copy(d, k, a, 0).wait_send()
                ring_copy(d, k, a, 1).wait_send()

            ring_copy(d, 4, a, d).wait_send()

    @pl.loop(1, 16)
    def _(i):
        other = (s + i) % 16
        col_copy(other).wait_send()
        colf_copy(0, other).wait_send()
        colf_copy(1, other).wait_send()


def local(tokens, query_weight, kv_weight, signs, cotangent):
    rows, cols = tokens.shape
    width = query_weight.shape[0]
    words = signs.shape[0]
    total = 16 * rows
    chunks = total // CHUNK
    dma = pltpu.SemaphoreType.DMA
    vmem = pltpu.VMEM
    scratch = [
        vmem((16, rows, cols), BF16),
        vmem((width, cols), BF16),
        vmem((width, HEAD), BF16),
        vmem((words, cols), jnp.int32),
        vmem((8 * BITS, HEAD), jnp.int32),
        vmem((words * BITS, cols), BF16),
        vmem((rows, cols), BF16),
        vmem((rows, cols), F32),
        vmem((rows, cols), F32),
        vmem((rows, HEAD), F32),
        vmem((total, cols), BF16),
        vmem((2, 16, rows, HEAD), BF16),
        vmem((2, 16, rows, HEAD), BF16),
        vmem((2, 2 * rows, HEAD), BF16),
        vmem((2, 2 * rows, HEAD), BF16),
        vmem((2, 2 * rows, HEAD), BF16),
        vmem((chunks, 2 * rows, CHUNK), F32),
        vmem((chunks, 2 * rows, CHUNK), F32),
        vmem((chunks, 2 * rows, CHUNK), F32),
        vmem((2 * rows, CHUNK), BF16),
        vmem((5, 2 * rows, HEAD), F32),
        vmem((2 * rows, HEAD), F32),
        vmem((2, total, cols // 2), BF16),
        dma((6,)),
        dma((16,)),
        dma((2, 4, 2, 2)),
        dma((2, 4, 2, 2)),
        dma((2,)),
        dma((2,)),
        dma((16,)),
        dma((16,)),
        dma((2, 16)),
        dma((2, 16)),
        dma((2,)),
        dma((2,)),
        dma((2,)),
        dma((7, 2)),
        dma((8, 2)),
        dma((16, 2)),
        dma((2, 7, 2)),
        dma((2, 8, 2)),
        dma((2, 16, 2)),
    ]
    return pl.pallas_call(
        kernel,
        out_shape=pltpu.VMEM((width // 16, cols), F32),
        in_specs=[pl.BlockSpec(memory_space=pl.ANY)] * 5,
        out_specs=pl.BlockSpec(memory_space=pltpu.VMEM),
        scratch_shapes=scratch,
        compiler_params=pltpu.CompilerParams(
            collective_id=0, has_side_effects=True, vmem_limit_bytes=60 * 1024 * 1024
        ),
        name="salience",
    )(tokens, query_weight, kv_weight, signs, cotangent)


def solution(mesh):
    placed = (P("seq", "head"), P(None, "head"), P(None, "head"), P(None, "head"), P("seq", "head"))
    return jax.shard_map(
        local, mesh=mesh, in_specs=placed, out_specs=P("seq", "head"), check_vma=False
    )
```

```python
import functools

import jax
import jax.numpy as jnp
from jax import lax
from jax.experimental import pallas as pl
from jax.experimental.pallas import tpu as pltpu
from jax.sharding import PartitionSpec as P

MESH = pl.DeviceIdType.MESH
BF16 = jnp.bfloat16
F32 = jnp.float32
BITS = 18
HEAD = 128
CHUNK = 768
LOG2E = 1.4426950408889634


def mm(a, b):
    return jnp.dot(a, b, preferred_element_type=F32)


def mm_bt(a, b):
    return lax.dot_general(a, b, (((1,), (1,)), ((), ())), preferred_element_type=F32)


def mm_at(a, b):
    return lax.dot_general(a, b, (((0,), (0,)), ((), ())), preferred_element_type=F32)


def kernel(
    tokens_hbm, weight_hbm, kv_weight_hbm, signs_hbm, cot_hbm, out,
    tok, weight, kv_weight, words, bitmask, sign, cot, acc_q, acc_t, acc_kv,
    col, kv, whole, qrows, trows, crows, buf_l, buf_t, buf_b, scores, stat, acc_u, upd,
    load_sem, w_sem, ring_s, ring_r, xh_s, xh_r, col_s, col_r, colf_s, colf_r,
    swap_s, swap_r, kvx_sem, kv_s, kv_f, kv_r, upd_s, upd_f, upd_r,
):
    rows, cols = tokens_hbm.shape
    half, quarter = rows // 2, rows // 4
    s = lax.axis_index("seq")
    h = lax.axis_index("head")
    xl, y, c = s // 8, (s // 2) % 4, s % 2
    xh, z = h // 8, h % 8
    parity = z % 2
    other_core = s + 1 - 2 * c

    def zdev(step):
        return (s, xh * 8 + (z + 8 + step) % 8)

    def rcopy(src, dst, send, recv, dev):
        return pltpu.make_async_remote_copy(
            src_ref=src, dst_ref=dst, send_sem=send, recv_sem=recv, device_id=dev, device_id_type=MESH
        )

    pair = 15 - s

    def part_rows(part):
        return pl.ds(pl.multiple_of(part * half, 16), half)

    def place_rows(src, part, count=half, shift=0):
        unit = (part + src // 8) % 2
        return pl.ds(pl.multiple_of((unit * 16 + src) * half + shift, 16), count)

    def feat_rows(f):
        return pl.ds(pl.multiple_of(f * cols, 512), cols)

    def block_of(a, zz):
        return ((xh + a) % 2) * 8 + (zz + 16) % 8

    barrier = pltpu.get_barrier_semaphore()
    xh_dev = (s, ((xh + 1) % 2) * 8 + z)
    for dev in (zdev(1), zdev(-1), xh_dev):
        pl.semaphore_signal(barrier, inc=1, device_id=dev, device_id_type=MESH)

    @pl.loop(1, 16)
    def _(i):
        pl.semaphore_signal(barrier, inc=1, device_id=((s + i) % 16, h), device_id_type=MESH)

    def w_load(f):
        return pltpu.make_async_copy(weight_hbm.at[feat_rows(f)], weight.at[feat_rows(f)], w_sem.at[f])

    tok_load = pltpu.make_async_copy(tokens_hbm.at[part_rows(0)], tok.at[h, part_rows(0)], load_sem.at[0])
    words_load = pltpu.make_async_copy(signs_hbm, words, load_sem.at[1])
    kvw_load = pltpu.make_async_copy(kv_weight_hbm, kv_weight, load_sem.at[2])
    cot_load = pltpu.make_async_copy(cot_hbm.at[part_rows(0)], cot.at[part_rows(0)], load_sem.at[3])
    tok_load.start()
    words_load.start()
    w_load(h).start()
    kvw_load.start()

    @pl.loop(1, 16)
    def _(i):
        w_load((h + i) % 16).start()

    cot_load.start()

    pl.semaphore_wait(barrier, 18)

    def chunk(f, part):
        return tok.at[f, part_rows(part)]

    def ring_copy(d, k, a, part):
        ref = chunk(block_of(a, z - (1 - 2 * d) * (k - 1)), part)
        return rcopy(
            ref, ref, ring_s.at[d, k - 1, a, part], ring_r.at[d, k - 1, a, part], zdev(1 - 2 * d)
        )

    def ring_arrival(d, k, a, part):
        ref = chunk(block_of(a, z - (1 - 2 * d) * k), part)
        return rcopy(
            ref, ref, ring_s.at[d, k - 1, a, part], ring_r.at[d, k - 1, a, part], zdev(1 - 2 * d)
        )

    def xh_copy(part):
        return rcopy(chunk(h, part), chunk(h, part), xh_s.at[part], xh_r.at[part], xh_dev)

    def xh_arrival(part):
        ref = chunk(block_of(1, z), part)
        return rcopy(ref, ref, xh_s.at[part], xh_r.at[part], xh_dev)

    def col_copy(f):
        return rcopy(
            chunk(f, parity),
            col.at[place_rows(s, parity)],
            col_s.at[f], col_r.at[s], (f, h),
        )

    def col_arrival(src):
        place = col.at[place_rows(src, parity)]
        return rcopy(place, place, col_s.at[src], col_r.at[src], (src, h))

    def col_local(part):
        return pltpu.make_async_copy(
            chunk(s, part), col.at[place_rows(s, part)], load_sem.at[4 + part]
        )

    def col_send(f):
        @pl.when(f != s)
        def _():
            col_copy(f).start()

    def col_keep(f):
        @pl.when(f == s)
        def _():
            col_local(0).start()
            col_local(1).start()

    tok_swap = rcopy(
        tokens_hbm.at[part_rows(1)], tok.at[h, part_rows(1)], swap_s.at[0], swap_r.at[0], (pair, h)
    )
    cot_swap = rcopy(
        cot_hbm.at[part_rows(1)], cot.at[part_rows(1)], swap_s.at[1], swap_r.at[1], (pair, h)
    )
    tok_swap.start()
    tok_load.wait()

    def own_send(part):
        xh_copy(part).start()
        ring_copy(0, 1, 0, part).start()
        ring_copy(1, 1, 0, part).start()

        @pl.when(part == parity)
        def _():
            col_send(h)

    own_send(0)
    acc_q[...] = jnp.zeros_like(acc_q)
    acc_t[...] = jnp.zeros_like(acc_t)
    acc_kv[...] = jnp.zeros_like(acc_kv)
    words_load.wait()
    sub = lax.broadcasted_iota(jnp.int32, (8, HEAD), 0)
    for k in range(BITS):
        shift = sub + (8 * k) % BITS
        shift = jnp.where(shift >= BITS, shift - BITS, shift)
        bitmask[8 * k : 8 * k + 8, :] = jnp.left_shift(jnp.ones_like(shift), shift)

    def decode_group(g):
        for lane in range(cols // HEAD):
            w8 = words[pl.ds(pl.multiple_of(g * 8, 8), 8), lane * HEAD : (lane + 1) * HEAD]
            for k2 in range(BITS // 2):
                parts = []
                for k in (2 * k2, 2 * k2 + 1):
                    first, last = 8 * k // BITS, (8 * k + 7) // BITS
                    word = jnp.broadcast_to(w8[first : first + 1], (8, HEAD))
                    if last != first:
                        later = jnp.broadcast_to(w8[last : last + 1], (8, HEAD))
                        word = jnp.where(sub >= BITS * last - 8 * k, later, word)
                    bit = word & bitmask[8 * k : 8 * k + 8, :]
                    parts.append(jnp.where(bit != 0, 1.0, -1.0).astype(F32))
                tile = jnp.concatenate(parts, axis=0).astype(BF16)
                at = pl.multiple_of(g * (8 * BITS) + 16 * k2, 16)
                sign[pl.ds(at, 16), lane * HEAD : (lane + 1) * HEAD] = tile

    def decode(f):
        low = f * cols // (8 * BITS)
        high = (f * cols + cols - 1) // (8 * BITS)

        @pl.loop(low, high + 1)
        def _(g):
            decode_group(g)

    def project_kv(f):
        acc_kv[...] += mm(tok[f], kv_weight[feat_rows(f), :])

    def project_q(f):
        w_load(f).wait()
        block = tok[f]
        acc_q[...] += mm(block, weight[feat_rows(f), :])
        acc_t[...] += mm(block, sign[feat_rows(f), :])

    def other_send(part):
        xh_arrival(part).wait_recv()
        ring_copy(0, 1, 1, part).start()
        ring_copy(1, 1, 1, part).start()

    other_send(0)
    tok_swap.wait_recv()
    own_send(1)
    col_keep(h)
    decode(h)
    other_send(1)
    cot_swap.start()
    col_send(block_of(1, z))
    col_keep(block_of(1, z))
    kvw_load.wait()
    project_kv(h)
    project_q(h)

    @pl.loop(0, 24)
    def _(m):
        k = m // 8 + 1
        part = (m // 4) % 2
        a = (m // 2) % 2
        d = m % 2
        ring_arrival(d, k, a, part).wait_recv()

        @pl.when((k < 3) | (part == d))
        def _():
            ring_copy(d, k + 1, a, part).start()

        f = block_of(a, z - (1 - 2 * d) * k)

        @pl.when(part == parity)
        def _():
            col_send(f)

        @pl.when(part == 0)
        def _():
            decode(f)

        @pl.when(part == 1)
        def _():
            col_keep(f)
            project_kv(f)
            project_q(f)

        @pl.when(m == 1)
        def _():
            decode(block_of(1, z))
            project_kv(block_of(1, z))
            project_q(block_of(1, z))

    decode(block_of(0, z + 4))
    decode(block_of(1, z + 4))

    @pl.loop(0, 2)
    def _(a):
        f = block_of(a, z + 4)
        ring_arrival(0, 4, a, 0).wait_recv()
        ring_arrival(1, 4, a, 1).wait_recv()
        project_kv(f)

    def colf_copy(d, src):
        place = col.at[place_rows(src, parity, quarter, d * quarter)]
        return rcopy(place, place, colf_s.at[d, src], colf_r.at[d, src], zdev(1 - 2 * d))

    def colf_arrival(d, src):
        place = col.at[place_rows(src, 1 - parity, quarter, d * quarter)]
        return rcopy(place, place, colf_s.at[d, src], colf_r.at[d, src], zdev(1 - 2 * d))

    away = (z + 8 - s % 8) % 8
    far = (away >= 3) & (away <= 5)

    x_peer = (xl + 1) % 2 * 8 + y * 2 + c

    def y_peer(step):
        return xl * 8 + (y + step) % 4 * 2 + c

    def xy_peer(step):
        return (xl + 1) % 2 * 8 + (y + step) % 4 * 2 + c

    class Gather:
        def __init__(self, place, send, fwd, recv):
            self.place, self.send, self.fwd, self.recv = place, send, fwd, recv

        def to(self, src, dev, i, p):
            ref = self.place(src, p)
            return rcopy(ref, ref, self.send.at[i, p], self.recv.at[src, p], (dev, h))

        def arrived(self, src, p):
            self.to(src, x_peer, 0, p).wait_recv()

        def share(self, src, p):
            ref = self.place(src, p)
            rcopy(ref, ref, self.fwd.at[src // 2, p], self.recv.at[src, p], (other_core, h)).start()

        def start(self, pieces=(0, 1)):
            def along_x():
                for p in pieces:
                    self.to(s, x_peer, 0, p).start()

            def along_y():
                for p in pieces:
                    for step in (1, 3, 2):
                        self.to(s, y_peer(step), step, p).start()
                    self.share(s, p)

            @pl.when(c == 0)
            def _():
                along_x()
                along_y()

            @pl.when(c == 1)
            def _():
                along_y()
                along_x()

        def middle(self, p):
            @pl.when(c == 0)
            def _():
                self.arrived(x_peer, p)
                for i, step in enumerate((1, 3, 2)):
                    self.to(x_peer, y_peer(step), 4 + i, p).start()
                self.share(x_peer, p)

            @pl.when(c == 1)
            def _():
                for i, step in enumerate((1, 3, 2)):
                    self.arrived(y_peer(step), p)
                    self.to(y_peer(step), x_peer, 4 + i, p).start()
                    self.share(y_peer(step), p)

        def end(self, p):
            @pl.when(c == 0)
            def _():
                for step in (1, 3, 2):
                    self.arrived(y_peer(step), p)
                    self.share(y_peer(step), p)

            @pl.when(c == 1)
            def _():
                self.arrived(x_peer, p)
                self.share(x_peer, p)

            for step in (1, 3, 2):
                self.arrived(xy_peer(step), p)
                self.share(xy_peer(step), p)

        def finish(self, p):
            for step in range(4):
                self.arrived(y_peer(step) + 1 - 2 * c, p)
                self.arrived(xy_peer(step) + 1 - 2 * c, p)

        def drain(self):
            for p in range(2):
                for i in range(7):
                    self.to(s, x_peer, i, p).wait_send()
                ref = self.place(s, p)
                for i in range(8):
                    rcopy(ref, ref, self.fwd.at[i, p], self.recv.at[s, p], (other_core, h)).wait_send()

    def cores(src):
        return [src, src + 1 - 2 * c]

    close = [other_core] + cores(y_peer(1)) + cores(y_peer(3)) + cores(x_peer)
    distant = cores(xy_peer(1)) + cores(xy_peer(3)) + cores(y_peer(2)) + cores(xy_peer(2))

    def col_forward(when, sources):
        @pl.when(when)
        def _():
            for src in sources:
                col_arrival(src).wait_recv()
                colf_copy(0, src).start()
                colf_copy(1, src).start()

    odd = h % 2
    kv[odd, s] = acc_kv[...].astype(BF16)
    kvx = rcopy(
        kv.at[odd, s], kv.at[odd, s], kvx_sem.at[0], kvx_sem.at[1], (s, h + 1 - 2 * odd)
    )
    kvx_arrival = rcopy(
        kv.at[1 - odd, s], kv.at[1 - odd, s], kvx_sem.at[0], kvx_sem.at[1], (s, h + 1 - 2 * odd)
    )
    kv_gather = Gather(lambda src, p: kv.at[(odd + p) % 2, src], kv_s, kv_f, kv_r)
    kvx.start()
    kv_gather.start((0,))

    @pl.loop(0, 2)
    def _(a):
        project_q(block_of(a, z + 4))

    kvx_arrival.wait_recv()
    kv_gather.start((1,))
    kv_gather.middle(0)

    cot_load.wait()
    cot_swap.wait_recv()
    heads = cols // HEAD
    def fill_rows(u):
        at = pl.ds(pl.multiple_of((u + xl) % 2 * half, 16), half)
        for j in range(heads):
            lanes = slice(j * HEAD, (j + 1) * HEAD)
            into = slice(j * half, (j + 1) * half)
            qrows[u, into, :] = acc_q[at, lanes].astype(BF16)
            trows[u, into, :] = acc_t[at, lanes].astype(BF16)
            crows[u, into, :] = cot[at, lanes]

    fill_rows(0)
    kv_gather.middle(1)
    kv_gather.end(0)

    @pl.loop(0, 2)
    def _(a):
        col_send(block_of(a, z + 4))
        col_keep(block_of(a, z + 4))

    fill_rows(1)
    kv_gather.end(1)
    col_forward(jnp.logical_not(far), close + distant)
    kv_gather.finish(0)
    kv_gather.finish(1)
    col_forward(far, close)

    low = lax.broadcasted_iota(jnp.int32, (rows, HEAD), 1) < HEAD // 2

    def turned(block):
        return jnp.concatenate([block[:, HEAD // 2 :], block[:, : HEAD // 2]], axis=1)

    @pl.loop(0, 16)
    def _(src):
        lower, upper = kv[0, src].astype(F32), kv[1, src].astype(F32)
        whole[0, src] = jnp.where(low, lower, turned(upper)).astype(BF16)
        whole[1, src] = jnp.where(low, turned(lower), upper).astype(BF16)

    scale = HEAD ** (-0.5)
    n_rows = heads * half
    pieces = CHUNK // half
    tiles = CHUNK // HEAD

    def attend(u, b, hook_sums, hook_half):
        count = (b + pieces) // pieces

        def load(j, which):
            parts = []
            for i in range(pieces // 2):
                owner = j * (pieces // 2) + i
                for src, at in ((owner, slice(0, half)), (15 - owner, slice(half, rows))):
                    parts.append(whole[which, src, at])
            return jnp.concatenate(parts, axis=0)

        keys, values = 0, 1
        runs = [slice(p * half, (p + 1) * half) for p in range(heads)]
        strips = [slice(q * HEAD, (q + 1) * HEAD) for q in range(tiles)]

        def logits_of(j, last):
            buf_l[j] = mm_bt(qrows[u], load(j, keys))
            if last:
                rel = lax.broadcasted_iota(jnp.int32, (half, CHUNK), 1) - lax.broadcasted_iota(
                    jnp.int32, (half, CHUNK), 0
                )
                seen = rel <= b * half - j * CHUNK
            for r in runs:
                if last:
                    buf_l[j, r, :] = jnp.where(seen, buf_l[j, r, :], -1e30)
                high = stat[0, r, :]
                for lanes in strips:
                    high = jnp.maximum(high, buf_l[j, r, lanes])
                stat[0, r, :] = high

        stat[0] = jnp.full((n_rows, HEAD), -1e30, F32)

        @pl.loop(0, count - 1)
        def _(j):
            logits_of(j, False)

        logits_of(count - 1, True)
        stat[0] = jnp.broadcast_to(jnp.max(stat[0], axis=1, keepdims=True), (n_rows, HEAD))
        for i in range(1, 5):
            stat[i] = jnp.zeros((n_rows, HEAD), F32)

        @pl.loop(0, count)
        def _(j):
            buf_t[j] = mm_bt(trows[u], load(j, keys))
            buf_b[j] = mm_bt(crows[u], load(j, values))
            for r in runs:
                top = stat[0, r, :]
                sums = [stat[i, r, :] for i in range(1, 5)]
                for lanes in strips:
                    e = jnp.exp2((buf_l[j, r, lanes] - top) * (scale * LOG2E))
                    buf_l[j, r, lanes] = e
                    back = buf_b[j, r, lanes]
                    et = e * buf_t[j, r, lanes]
                    for i, term in enumerate((e, et, e * back, et * back)):
                        sums[i] += term
                for i in range(4):
                    stat[i + 1, r, :] = sums[i]

        hook_sums()
        sums = [jnp.sum(stat[i], axis=1, keepdims=True) for i in range(1, 5)]
        inverse = 1.0 / sums[0]
        middle = sums[1] * inverse
        delta = sums[2] * inverse
        delta_t = sums[3] * inverse - middle * delta
        for i, value in enumerate((middle, delta, delta_t)):
            stat[i] = jnp.broadcast_to(value, (n_rows, HEAD))
        acc_u[...] = jnp.zeros_like(acc_u)

        factor = inverse * (scale * scale)
        for p in range(2):
            both = slice(p * n_rows // 2, (p + 1) * n_rows // 2)

            @pl.loop(0, count)
            def _(j):
                for r in runs[2 * p : 2 * p + 2]:
                    middle, delta, delta_t = stat[0, r, :], stat[1, r, :], stat[2, r, :]
                    for lanes in strips:
                        score = buf_l[j, r, lanes] * (
                            (buf_t[j, r, lanes] - middle) * (buf_b[j, r, lanes] - delta) - delta_t
                        )
                        scores[r, lanes] = score.astype(BF16)
                acc_u[both, :] += mm(scores[both, :], load(j, keys))

            update = (acc_u[both, :] * factor[both]).astype(BF16)
            upd[p, upd_rows(u, s), :] = jnp.concatenate([update[:half], update[half:]], axis=1)
            hook_half(p)

    def upd_rows(u, src):
        return pl.ds(pl.multiple_of((u * 16 + src) * half, 16), half)

    early = jnp.minimum(2 * s, 31 - 2 * s)
    def update_gather(u):
        return Gather(
            lambda src, p: upd.at[p, upd_rows(u, src)], upd_s.at[u], upd_f.at[u], upd_r.at[u]
        )

    gathers = [update_gather(0), update_gather(1)]

    @pl.loop(0, 2)
    def _(u):
        def first_middle():
            col_forward(far & (u == 0), distant)

            @pl.when(u == 1)
            def _():
                gathers[0].middle(0)
                gathers[0].middle(1)

        attend(
            u, early + u * (31 - 2 * early), first_middle, lambda p: update_gather(u).start((p,))
        )

    gathers[0].end(0)
    gathers[1].middle(0)
    gathers[0].end(1)
    gathers[1].middle(1)
    gathers[0].finish(0)
    gathers[0].finish(1)

    @pl.loop(1, 16)
    def _(i):
        src = (s + i) % 16
        colf_arrival(0, src).wait_recv()
        colf_arrival(1, src).wait_recv()

    col_local(0).wait()
    col_local(1).wait()
    side = 16 * half

    width = cols // 2

    def hessian(u, t, p):
        run = slice(u * side, (u + 1) * side)
        return mm_at(col[run, t * 256 : (t + 1) * 256], upd[p, run, :])

    places = [
        (t, p, slice(t * 256, (t + 1) * 256), slice(p * width, (p + 1) * width))
        for p in range(2)
        for t in range(cols // 256)
    ]
    for t, p, r, lanes in places:
        out[r, lanes] = hessian(0, t, p)
    for p in range(2):
        gathers[1].end(p)
    for p in range(2):
        gathers[1].finish(p)
        for t, q, r, lanes in places:
            if p == q:
                own = sign[pl.ds(pl.multiple_of(s * cols + t * 256, 256), 256), lanes]
                out[r, lanes] = (out[r, lanes] + hessian(1, t, p)) * own.astype(F32)

    for gather in [kv_gather] + gathers:
        gather.drain()
    tok_swap.wait_send()
    cot_swap.wait_send()
    kvx.wait_send()
    for part in range(2):
        xh_copy(part).wait_send()

    @pl.loop(0, 2)
    def _(d):
        @pl.loop(0, 2)
        def _(a):
            @pl.loop(1, 4)
            def _(k):
                ring_copy(d, k, a, 0).wait_send()
                ring_copy(d, k, a, 1).wait_send()

            ring_copy(d, 4, a, d).wait_send()

    @pl.loop(1, 16)
    def _(i):
        other = (s + i) % 16
        col_copy(other).wait_send()
        colf_copy(0, other).wait_send()
        colf_copy(1, other).wait_send()


def local(tokens, query_weight, kv_weight, signs, cotangent):
    rows, cols = tokens.shape
    width = query_weight.shape[0]
    words = signs.shape[0]
    total = 16 * rows
    chunks = total // CHUNK
    dma = pltpu.SemaphoreType.DMA
    vmem = pltpu.VMEM
    scratch = [
        vmem((16, rows, cols), BF16),
        vmem((width, cols), BF16),
        vmem((width, HEAD), BF16),
        vmem((words, cols), jnp.int32),
        vmem((8 * BITS, HEAD), jnp.int32),
        vmem((words * BITS, cols), BF16),
        vmem((rows, cols), BF16),
        vmem((rows, cols), F32),
        vmem((rows, cols), F32),
        vmem((rows, HEAD), F32),
        vmem((total, cols), BF16),
        vmem((2, 16, rows, HEAD), BF16),
        vmem((2, 16, rows, HEAD), BF16),
        vmem((2, 2 * rows, HEAD), BF16),
        vmem((2, 2 * rows, HEAD), BF16),
        vmem((2, 2 * rows, HEAD), BF16),
        vmem((chunks, 2 * rows, CHUNK), F32),
        vmem((chunks, 2 * rows, CHUNK), F32),
        vmem((chunks, 2 * rows, CHUNK), F32),
        vmem((2 * rows, CHUNK), BF16),
        vmem((5, 2 * rows, HEAD), F32),
        vmem((2 * rows, HEAD), F32),
        vmem((2, total, cols // 2), BF16),
        dma((6,)),
        dma((16,)),
        dma((2, 4, 2, 2)),
        dma((2, 4, 2, 2)),
        dma((2,)),
        dma((2,)),
        dma((16,)),
        dma((16,)),
        dma((2, 16)),
        dma((2, 16)),
        dma((2,)),
        dma((2,)),
        dma((2,)),
        dma((7, 2)),
        dma((8, 2)),
        dma((16, 2)),
        dma((2, 7, 2)),
        dma((2, 8, 2)),
        dma((2, 16, 2)),
    ]
    return pl.pallas_call(
        kernel,
        out_shape=pltpu.VMEM((width // 16, cols), F32),
        in_specs=[pl.BlockSpec(memory_space=pl.ANY)] * 5,
        out_specs=pl.BlockSpec(memory_space=pltpu.VMEM),
        scratch_shapes=scratch,
        compiler_params=pltpu.CompilerParams(
            collective_id=0, has_side_effects=True, vmem_limit_bytes=60 * 1024 * 1024
        ),
        name="salience",
    )(tokens, query_weight, kv_weight, signs, cotangent)


def solution(mesh):
    placed = (P("seq", "head"), P(None, "head"), P(None, "head"), P(None, "head"), P("seq", "head"))
    return jax.shard_map(
        local, mesh=mesh, in_specs=placed, out_specs=P("seq", "head"), check_vma=False
    )
```

```python
import functools

import jax
import jax.numpy as jnp
from jax import lax
from jax.experimental import pallas as pl
from jax.experimental.pallas import tpu as pltpu
from jax.sharding import PartitionSpec as P

MESH = pl.DeviceIdType.MESH
BF16 = jnp.bfloat16
F32 = jnp.float32
BITS = 18
HEAD = 128
CHUNK = 768
LOG2E = 1.4426950408889634


def mm(a, b):
    return jnp.dot(a, b, preferred_element_type=F32)


def mm_bt(a, b):
    return lax.dot_general(a, b, (((1,), (1,)), ((), ())), preferred_element_type=F32)


def mm_at(a, b):
    return lax.dot_general(a, b, (((0,), (0,)), ((), ())), preferred_element_type=F32)


def kernel(
    tokens_hbm, weight_hbm, kv_weight_hbm, signs_hbm, cot_hbm, out,
    tok, weight, kv_weight, words, bitmask, sign, cot, acc_q, acc_t, acc_kv,
    col, kv, whole, qrows, trows, crows, buf_l, buf_t, buf_b, scores, stat, acc_u, upd,
    load_sem, w_sem, ring_s, ring_r, xh_s, xh_r, col_s, col_r, colf_s, colf_r,
    swap_s, swap_r, kvx_sem, kv_s, kv_f, kv_r, upd_s, upd_f, upd_r,
):
    rows, cols = tokens_hbm.shape
    half, quarter = rows // 2, rows // 4
    s = lax.axis_index("seq")
    h = lax.axis_index("head")
    xl, y, c = s // 8, (s // 2) % 4, s % 2
    xh, z = h // 8, h % 8
    parity = z % 2
    other_core = s + 1 - 2 * c

    def zdev(step):
        return (s, xh * 8 + (z + 8 + step) % 8)

    def rcopy(src, dst, send, recv, dev):
        return pltpu.make_async_remote_copy(
            src_ref=src, dst_ref=dst, send_sem=send, recv_sem=recv, device_id=dev, device_id_type=MESH
        )

    pair = 15 - s

    def part_rows(part):
        return pl.ds(pl.multiple_of(part * half, 16), half)

    def place_rows(src, part, count=half, shift=0):
        unit = (part + src // 8) % 2
        return pl.ds(pl.multiple_of((unit * 16 + src) * half + shift, 16), count)

    def feat_rows(f):
        return pl.ds(pl.multiple_of(f * cols, 512), cols)

    def block_of(a, zz):
        return ((xh + a) % 2) * 8 + (zz + 16) % 8

    barrier = pltpu.get_barrier_semaphore()
    xh_dev = (s, ((xh + 1) % 2) * 8 + z)
    for dev in (zdev(1), zdev(-1), xh_dev):
        pl.semaphore_signal(barrier, inc=1, device_id=dev, device_id_type=MESH)

    @pl.loop(1, 16)
    def _(i):
        pl.semaphore_signal(barrier, inc=1, device_id=((s + i) % 16, h), device_id_type=MESH)

    def w_load(f):
        return pltpu.make_async_copy(weight_hbm.at[feat_rows(f)], weight.at[feat_rows(f)], w_sem.at[f])

    tok_load = pltpu.make_async_copy(tokens_hbm.at[part_rows(0)], tok.at[h, part_rows(0)], load_sem.at[0])
    words_load = pltpu.make_async_copy(signs_hbm, words, load_sem.at[1])
    kvw_load = pltpu.make_async_copy(kv_weight_hbm, kv_weight, load_sem.at[2])
    cot_load = pltpu.make_async_copy(cot_hbm.at[part_rows(0)], cot.at[part_rows(0)], load_sem.at[3])
    tok_load.start()
    words_load.start()
    w_load(h).start()
    kvw_load.start()

    @pl.loop(1, 16)
    def _(i):
        w_load((h + i) % 16).start()

    cot_load.start()

    pl.semaphore_wait(barrier, 18)

    def chunk(f, part):
        return tok.at[f, part_rows(part)]

    def ring_copy(d, k, a, part):
        ref = chunk(block_of(a, z - (1 - 2 * d) * (k - 1)), part)
        return rcopy(
            ref, ref, ring_s.at[d, k - 1, a, part], ring_r.at[d, k - 1, a, part], zdev(1 - 2 * d)
        )

    def ring_arrival(d, k, a, part):
        ref = chunk(block_of(a, z - (1 - 2 * d) * k), part)
        return rcopy(
            ref, ref, ring_s.at[d, k - 1, a, part], ring_r.at[d, k - 1, a, part], zdev(1 - 2 * d)
        )

    def xh_copy(part):
        return rcopy(chunk(h, part), chunk(h, part), xh_s.at[part], xh_r.at[part], xh_dev)

    def xh_arrival(part):
        ref = chunk(block_of(1, z), part)
        return rcopy(ref, ref, xh_s.at[part], xh_r.at[part], xh_dev)

    def col_copy(f):
        return rcopy(
            chunk(f, parity),
            col.at[place_rows(s, parity)],
            col_s.at[f], col_r.at[s], (f, h),
        )

    def col_arrival(src):
        place = col.at[place_rows(src, parity)]
        return rcopy(place, place, col_s.at[src], col_r.at[src], (src, h))

    def col_local(part):
        return pltpu.make_async_copy(
            chunk(s, part), col.at[place_rows(s, part)], load_sem.at[4 + part]
        )

    def col_send(f):
        @pl.when(f != s)
        def _():
            col_copy(f).start()

    def col_keep(f):
        @pl.when(f == s)
        def _():
            col_local(0).start()
            col_local(1).start()

    tok_swap = rcopy(
        tokens_hbm.at[part_rows(1)], tok.at[h, part_rows(1)], swap_s.at[0], swap_r.at[0], (pair, h)
    )
    cot_swap = rcopy(
        cot_hbm.at[part_rows(1)], cot.at[part_rows(1)], swap_s.at[1], swap_r.at[1], (pair, h)
    )
    tok_swap.start()
    tok_load.wait()

    def own_send(part):
        xh_copy(part).start()
        ring_copy(0, 1, 0, part).start()
        ring_copy(1, 1, 0, part).start()

        @pl.when(part == parity)
        def _():
            col_send(h)

    own_send(0)
    acc_q[...] = jnp.zeros_like(acc_q)
    acc_t[...] = jnp.zeros_like(acc_t)
    acc_kv[...] = jnp.zeros_like(acc_kv)
    words_load.wait()
    sub = lax.broadcasted_iota(jnp.int32, (8, HEAD), 0)
    for k in range(BITS):
        shift = sub + (8 * k) % BITS
        shift = jnp.where(shift >= BITS, shift - BITS, shift)
        bitmask[8 * k : 8 * k + 8, :] = jnp.left_shift(jnp.ones_like(shift), shift)

    def decode_group(g):
        for lane in range(cols // HEAD):
            w8 = words[pl.ds(pl.multiple_of(g * 8, 8), 8), lane * HEAD : (lane + 1) * HEAD]
            for k2 in range(BITS // 2):
                parts = []
                for k in (2 * k2, 2 * k2 + 1):
                    first, last = 8 * k // BITS, (8 * k + 7) // BITS
                    word = jnp.broadcast_to(w8[first : first + 1], (8, HEAD))
                    if last != first:
                        later = jnp.broadcast_to(w8[last : last + 1], (8, HEAD))
                        word = jnp.where(sub >= BITS * last - 8 * k, later, word)
                    bit = word & bitmask[8 * k : 8 * k + 8, :]
                    parts.append(jnp.where(bit != 0, 1.0, -1.0).astype(F32))
                tile = jnp.concatenate(parts, axis=0).astype(BF16)
                at = pl.multiple_of(g * (8 * BITS) + 16 * k2, 16)
                sign[pl.ds(at, 16), lane * HEAD : (lane + 1) * HEAD] = tile

    def decode(f):
        low = f * cols // (8 * BITS)
        high = (f * cols + cols - 1) // (8 * BITS)

        @pl.loop(low, high + 1)
        def _(g):
            decode_group(g)

    def project_kv(f):
        acc_kv[...] += mm(tok[f], kv_weight[feat_rows(f), :])

    def project_q(f):
        w_load(f).wait()
        block = tok[f]
        acc_q[...] += mm(block, weight[feat_rows(f), :])
        acc_t[...] += mm(block, sign[feat_rows(f), :])

    def other_send(part):
        xh_arrival(part).wait_recv()
        ring_copy(0, 1, 1, part).start()
        ring_copy(1, 1, 1, part).start()

    other_send(0)
    tok_swap.wait_recv()
    own_send(1)
    col_keep(h)
    decode(h)
    other_send(1)
    cot_swap.start()
    col_send(block_of(1, z))
    col_keep(block_of(1, z))
    kvw_load.wait()
    project_kv(h)
    project_q(h)

    @pl.loop(0, 24)
    def _(m):
        k = m // 8 + 1
        part = (m // 4) % 2
        a = (m // 2) % 2
        d = m % 2
        ring_arrival(d, k, a, part).wait_recv()

        @pl.when((k < 3) | (part == d))
        def _():
            ring_copy(d, k + 1, a, part).start()

        f = block_of(a, z - (1 - 2 * d) * k)

        @pl.when(part == parity)
        def _():
            col_send(f)

        @pl.when(part == 0)
        def _():
            decode(f)

        @pl.when(part == 1)
        def _():
            col_keep(f)
            project_kv(f)
            project_q(f)

        @pl.when(m == 1)
        def _():
            decode(block_of(1, z))
            project_kv(block_of(1, z))
            project_q(block_of(1, z))

    decode(block_of(0, z + 4))
    decode(block_of(1, z + 4))

    @pl.loop(0, 2)
    def _(a):
        f = block_of(a, z + 4)
        ring_arrival(0, 4, a, 0).wait_recv()
        ring_arrival(1, 4, a, 1).wait_recv()
        project_kv(f)

    def colf_copy(d, src):
        place = col.at[place_rows(src, parity, quarter, d * quarter)]
        return rcopy(place, place, colf_s.at[d, src], colf_r.at[d, src], zdev(1 - 2 * d))

    def colf_arrival(d, src):
        place = col.at[place_rows(src, 1 - parity, quarter, d * quarter)]
        return rcopy(place, place, colf_s.at[d, src], colf_r.at[d, src], zdev(1 - 2 * d))

    away = (z + 8 - s % 8) % 8
    far = (away >= 3) & (away <= 5)

    x_peer = (xl + 1) % 2 * 8 + y * 2 + c

    def y_peer(step):
        return xl * 8 + (y + step) % 4 * 2 + c

    def xy_peer(step):
        return (xl + 1) % 2 * 8 + (y + step) % 4 * 2 + c

    class Gather:
        def __init__(self, place, send, fwd, recv):
            self.place, self.send, self.fwd, self.recv = place, send, fwd, recv

        def to(self, src, dev, i, p):
            ref = self.place(src, p)
            return rcopy(ref, ref, self.send.at[i, p], self.recv.at[src, p], (dev, h))

        def arrived(self, src, p):
            self.to(src, x_peer, 0, p).wait_recv()

        def share(self, src, p):
            ref = self.place(src, p)
            rcopy(ref, ref, self.fwd.at[src // 2, p], self.recv.at[src, p], (other_core, h)).start()

        def start(self, pieces=(0, 1)):
            def along_x():
                for p in pieces:
                    self.to(s, x_peer, 0, p).start()

            def along_y():
                for p in pieces:
                    for step in (1, 3, 2):
                        self.to(s, y_peer(step), step, p).start()
                    self.share(s, p)

            @pl.when(c == 0)
            def _():
                along_x()
                along_y()

            @pl.when(c == 1)
            def _():
                along_y()
                along_x()

        def middle(self, p):
            @pl.when(c == 0)
            def _():
                self.arrived(x_peer, p)
                for i, step in enumerate((1, 3, 2)):
                    self.to(x_peer, y_peer(step), 4 + i, p).start()
                self.share(x_peer, p)

            @pl.when(c == 1)
            def _():
                for i, step in enumerate((1, 3, 2)):
                    self.arrived(y_peer(step), p)
                    self.to(y_peer(step), x_peer, 4 + i, p).start()
                    self.share(y_peer(step), p)

        def end(self, p):
            @pl.when(c == 0)
            def _():
                for step in (1, 3, 2):
                    self.arrived(y_peer(step), p)
                    self.share(y_peer(step), p)

            @pl.when(c == 1)
            def _():
                self.arrived(x_peer, p)
                self.share(x_peer, p)

            for step in (1, 3, 2):
                self.arrived(xy_peer(step), p)
                self.share(xy_peer(step), p)

        def finish(self, p):
            for step in range(4):
                self.arrived(y_peer(step) + 1 - 2 * c, p)
                self.arrived(xy_peer(step) + 1 - 2 * c, p)

        def drain(self):
            for p in range(2):
                for i in range(7):
                    self.to(s, x_peer, i, p).wait_send()
                ref = self.place(s, p)
                for i in range(8):
                    rcopy(ref, ref, self.fwd.at[i, p], self.recv.at[s, p], (other_core, h)).wait_send()

    def cores(src):
        return [src, src + 1 - 2 * c]

    close = [other_core] + cores(y_peer(1)) + cores(y_peer(3)) + cores(x_peer)
    distant = cores(xy_peer(1)) + cores(xy_peer(3)) + cores(y_peer(2)) + cores(xy_peer(2))

    def col_forward(when, sources):
        @pl.when(when)
        def _():
            for src in sources:
                col_arrival(src).wait_recv()
                colf_copy(0, src).start()
                colf_copy(1, src).start()

    odd = h % 2
    kv[odd, s] = acc_kv[...].astype(BF16)
    kvx = rcopy(
        kv.at[odd, s], kv.at[odd, s], kvx_sem.at[0], kvx_sem.at[1], (s, h + 1 - 2 * odd)
    )
    kvx_arrival = rcopy(
        kv.at[1 - odd, s], kv.at[1 - odd, s], kvx_sem.at[0], kvx_sem.at[1], (s, h + 1 - 2 * odd)
    )
    kv_gather = Gather(lambda src, p: kv.at[(odd + p) % 2, src], kv_s, kv_f, kv_r)
    kvx.start()
    kv_gather.start((0,))

    @pl.loop(0, 2)
    def _(a):
        project_q(block_of(a, z + 4))

    kvx_arrival.wait_recv()
    kv_gather.start((1,))
    kv_gather.middle(0)

    cot_load.wait()
    cot_swap.wait_recv()
    heads = cols // HEAD
    def fill_rows(u):
        at = pl.ds(pl.multiple_of((u + xl) % 2 * half, 16), half)
        for j in range(heads):
            lanes = slice(j * HEAD, (j + 1) * HEAD)
            into = slice(j * half, (j + 1) * half)
            qrows[u, into, :] = acc_q[at, lanes].astype(BF16)
            trows[u, into, :] = acc_t[at, lanes].astype(BF16)
            crows[u, into, :] = cot[at, lanes]

    fill_rows(0)
    kv_gather.middle(1)
    kv_gather.end(0)

    @pl.loop(0, 2)
    def _(a):
        col_send(block_of(a, z + 4))
        col_keep(block_of(a, z + 4))

    fill_rows(1)

    tok_swap.wait_send()
    cot_swap.wait_send()
    kvx.wait_send()
    for part in range(2):
        xh_copy(part).wait_send()

    @pl.loop(0, 2)
    def _(d):
        @pl.loop(0, 2)
        def _(a):
            @pl.loop(1, 4)
            def _(k):
                ring_copy(d, k, a, 0).wait_send()
                ring_copy(d, k, a, 1).wait_send()

            ring_copy(d, 4, a, d).wait_send()

    kv_gather.end(1)
    col_forward(jnp.logical_not(far), close + distant)
    kv_gather.finish(0)
    kv_gather.finish(1)
    col_forward(far, close)

    low = lax.broadcasted_iota(jnp.int32, (rows, HEAD), 1) < HEAD // 2

    def turned(block):
        return jnp.concatenate([block[:, HEAD // 2 :], block[:, : HEAD // 2]], axis=1)

    @pl.loop(0, 16)
    def _(src):
        lower, upper = kv[0, src].astype(F32), kv[1, src].astype(F32)
        whole[0, src] = jnp.where(low, lower, turned(upper)).astype(BF16)
        whole[1, src] = jnp.where(low, turned(lower), upper).astype(BF16)

    scale = HEAD ** (-0.5)
    n_rows = heads * half
    pieces = CHUNK // half
    tiles = CHUNK // HEAD

    def attend(u, b, hook_sums, hook_half):
        count = (b + pieces) // pieces

        def load(j, which):
            parts = []
            for i in range(pieces // 2):
                owner = j * (pieces // 2) + i
                for src, at in ((owner, slice(0, half)), (15 - owner, slice(half, rows))):
                    parts.append(whole[which, src, at])
            return jnp.concatenate(parts, axis=0)

        keys, values = 0, 1
        runs = [slice(p * half, (p + 1) * half) for p in range(heads)]
        strips = [slice(q * HEAD, (q + 1) * HEAD) for q in range(tiles)]

        def logits_of(j, last):
            buf_l[j] = mm_bt(qrows[u], load(j, keys))
            if last:
                rel = lax.broadcasted_iota(jnp.int32, (half, CHUNK), 1) - lax.broadcasted_iota(
                    jnp.int32, (half, CHUNK), 0
                )
                seen = rel <= b * half - j * CHUNK
            for r in runs:
                if last:
                    buf_l[j, r, :] = jnp.where(seen, buf_l[j, r, :], -1e30)
                high = stat[0, r, :]
                for lanes in strips:
                    high = jnp.maximum(high, buf_l[j, r, lanes])
                stat[0, r, :] = high

        stat[0] = jnp.full((n_rows, HEAD), -1e30, F32)

        @pl.loop(0, count - 1)
        def _(j):
            logits_of(j, False)

        logits_of(count - 1, True)
        stat[0] = jnp.broadcast_to(jnp.max(stat[0], axis=1, keepdims=True), (n_rows, HEAD))
        for i in range(1, 5):
            stat[i] = jnp.zeros((n_rows, HEAD), F32)

        @pl.loop(0, count)
        def _(j):
            buf_t[j] = mm_bt(trows[u], load(j, keys))
            buf_b[j] = mm_bt(crows[u], load(j, values))
            for r in runs:
                top = stat[0, r, :]
                sums = [stat[i, r, :] for i in range(1, 5)]
                for lanes in strips:
                    e = jnp.exp2((buf_l[j, r, lanes] - top) * (scale * LOG2E))
                    buf_l[j, r, lanes] = e
                    back = buf_b[j, r, lanes]
                    et = e * buf_t[j, r, lanes]
                    for i, term in enumerate((e, et, e * back, et * back)):
                        sums[i] += term
                for i in range(4):
                    stat[i + 1, r, :] = sums[i]

        hook_sums()
        sums = [jnp.sum(stat[i], axis=1, keepdims=True) for i in range(1, 5)]
        inverse = 1.0 / sums[0]
        middle = sums[1] * inverse
        delta = sums[2] * inverse
        delta_t = sums[3] * inverse - middle * delta
        for i, value in enumerate((middle, delta, delta_t)):
            stat[i] = jnp.broadcast_to(value, (n_rows, HEAD))
        acc_u[...] = jnp.zeros_like(acc_u)

        factor = inverse * (scale * scale)
        for p in range(2):
            both = slice(p * n_rows // 2, (p + 1) * n_rows // 2)

            @pl.loop(0, count)
            def _(j):
                for r in runs[2 * p : 2 * p + 2]:
                    middle, delta, delta_t = stat[0, r, :], stat[1, r, :], stat[2, r, :]
                    for lanes in strips:
                        score = buf_l[j, r, lanes] * (
                            (buf_t[j, r, lanes] - middle) * (buf_b[j, r, lanes] - delta) - delta_t
                        )
                        scores[r, lanes] = score.astype(BF16)
                acc_u[both, :] += mm(scores[both, :], load(j, keys))

            update = (acc_u[both, :] * factor[both]).astype(BF16)
            upd[p, upd_rows(u, s), :] = jnp.concatenate([update[:half], update[half:]], axis=1)
            hook_half(p)

    def upd_rows(u, src):
        return pl.ds(pl.multiple_of((u * 16 + src) * half, 16), half)

    early = jnp.minimum(2 * s, 31 - 2 * s)
    def update_gather(u):
        return Gather(
            lambda src, p: upd.at[p, upd_rows(u, src)], upd_s.at[u], upd_f.at[u], upd_r.at[u]
        )

    gathers = [update_gather(0), update_gather(1)]

    @pl.loop(0, 2)
    def _(u):
        def first_middle():
            col_forward(far & (u == 0), distant)

            @pl.when(u == 1)
            def _():
                gathers[0].middle(0)
                gathers[0].middle(1)

        attend(
            u, early + u * (31 - 2 * early), first_middle, lambda p: update_gather(u).start((p,))
        )

    gathers[0].end(0)
    gathers[1].middle(0)
    gathers[0].end(1)
    gathers[1].middle(1)
    gathers[0].finish(0)
    gathers[0].finish(1)

    @pl.loop(1, 16)
    def _(i):
        src = (s + i) % 16
        colf_arrival(0, src).wait_recv()
        colf_arrival(1, src).wait_recv()

    col_local(0).wait()
    col_local(1).wait()
    side = 16 * half

    width = cols // 2

    def hessian(u, t, p):
        run = slice(u * side, (u + 1) * side)
        return mm_at(col[run, t * 256 : (t + 1) * 256], upd[p, run, :])

    places = [
        (t, p, slice(t * 256, (t + 1) * 256), slice(p * width, (p + 1) * width))
        for p in range(2)
        for t in range(cols // 256)
    ]
    for t, p, r, lanes in places:
        out[r, lanes] = hessian(0, t, p)

    kv_gather.drain()
    gathers[0].drain()

    @pl.loop(1, 16)
    def _(i):
        other = (s + i) % 16
        col_copy(other).wait_send()
        colf_copy(0, other).wait_send()
        colf_copy(1, other).wait_send()

    for p in range(2):
        gathers[1].end(p)
    for p in range(2):
        gathers[1].finish(p)
        for t, q, r, lanes in places:
            if p == q:
                own = sign[pl.ds(pl.multiple_of(s * cols + t * 256, 256), 256), lanes]
                out[r, lanes] = (out[r, lanes] + hessian(1, t, p)) * own.astype(F32)

    gathers[1].drain()


def local(tokens, query_weight, kv_weight, signs, cotangent):
    rows, cols = tokens.shape
    width = query_weight.shape[0]
    words = signs.shape[0]
    total = 16 * rows
    chunks = total // CHUNK
    dma = pltpu.SemaphoreType.DMA
    vmem = pltpu.VMEM
    scratch = [
        vmem((16, rows, cols), BF16),
        vmem((width, cols), BF16),
        vmem((width, HEAD), BF16),
        vmem((words, cols), jnp.int32),
        vmem((8 * BITS, HEAD), jnp.int32),
        vmem((words * BITS, cols), BF16),
        vmem((rows, cols), BF16),
        vmem((rows, cols), F32),
        vmem((rows, cols), F32),
        vmem((rows, HEAD), F32),
        vmem((total, cols), BF16),
        vmem((2, 16, rows, HEAD), BF16),
        vmem((2, 16, rows, HEAD), BF16),
        vmem((2, 2 * rows, HEAD), BF16),
        vmem((2, 2 * rows, HEAD), BF16),
        vmem((2, 2 * rows, HEAD), BF16),
        vmem((chunks, 2 * rows, CHUNK), F32),
        vmem((chunks, 2 * rows, CHUNK), F32),
        vmem((chunks, 2 * rows, CHUNK), F32),
        vmem((2 * rows, CHUNK), BF16),
        vmem((5, 2 * rows, HEAD), F32),
        vmem((2 * rows, HEAD), F32),
        vmem((2, total, cols // 2), BF16),
        dma((6,)),
        dma((16,)),
        dma((2, 4, 2, 2)),
        dma((2, 4, 2, 2)),
        dma((2,)),
        dma((2,)),
        dma((16,)),
        dma((16,)),
        dma((2, 16)),
        dma((2, 16)),
        dma((2,)),
        dma((2,)),
        dma((2,)),
        dma((7, 2)),
        dma((8, 2)),
        dma((16, 2)),
        dma((2, 7, 2)),
        dma((2, 8, 2)),
        dma((2, 16, 2)),
    ]
    return pl.pallas_call(
        kernel,
        out_shape=pltpu.VMEM((width // 16, cols), F32),
        in_specs=[pl.BlockSpec(memory_space=pl.ANY)] * 5,
        out_specs=pl.BlockSpec(memory_space=pltpu.VMEM),
        scratch_shapes=scratch,
        compiler_params=pltpu.CompilerParams(
            collective_id=0, has_side_effects=True, vmem_limit_bytes=60 * 1024 * 1024
        ),
        name="salience",
    )(tokens, query_weight, kv_weight, signs, cotangent)


def solution(mesh):
    placed = (P("seq", "head"), P(None, "head"), P(None, "head"), P(None, "head"), P("seq", "head"))
    return jax.shard_map(
        local, mesh=mesh, in_specs=placed, out_specs=P("seq", "head"), check_vma=False
    )
```
